256 devices in a mesh: row: 8 (over z), col: 32 (over x, y, core).
Axes of the slice: x: 4, y: 4, z: 8, core: 2. Of those that a mesh axis runs over, the one named last changes fastest.
Arguments:
- hamiltonian: bfloat16 [32768, 32768], P('row', 'col'), may hold values from -0.5 to 0.5, as said below
- start_block: float32 [32768, 128], P('row'), may hold values from -120 to 120
- spectral_bound: float32 [1], replicated, may hold values from 1.25 to 1.45
Outputs:
- basis: float32 [32768, 128], P(('row', 'col'))
- r_factor: float32 [128, 128], replicated
The draws below stay inside these ranges and needn't reach their ends.
Inputs may be any that keep to these rules, and one draw needn't show every extreme that they name: hamiltonian is exactly symmetric.
All inputs are finite; a program needn't handle non-finite values.
Results may differ from the reference program's by a relative error of at most 0.005.
Values may be sent and summed in bfloat16 or wider, within the bound.
No kernel may reach another device: no remote copies, remote signals or barrier semaphores. Data moves between devices by JAX's collectives and lax.ppermute only.
A program may use at most 64 MiB of HBM per device.

```python
import math
import jax
import jax.numpy as jnp
from jax import lax

N = 32768
K = 128
DEG = 4


def draw_hamiltonian(key, part):
    key = jax.random.fold_in(key, 11)
    key_main, key_diag = jax.random.split(key)
    entries = jax.random.truncated_normal(key_main, -5.0, 5.0, (N, N), jnp.float32)
    symmetric = (entries + entries.T) * (0.5 / math.sqrt(2.0 * N))
    energies = jax.random.uniform(key_diag, (N,), jnp.float32, -0.3, 0.3)
    return (symmetric + jnp.diag(energies)).astype(jnp.bfloat16)


def draw_start_block(key, part):
    key = jax.random.fold_in(key, 23)
    key_main, key_rows, key_cols = jax.random.split(key, 3)
    entries = jax.random.truncated_normal(key_main, -5.0, 5.0, (N, K), jnp.float32)
    position = jnp.arange(N, dtype=jnp.float32) / N
    ramp = jnp.exp(math.log(3.0) * position)
    row_scales = ramp * jnp.exp(jax.random.uniform(key_rows, (N,), jnp.float32, 0.0, math.log(2.0)))
    col_scales = jnp.exp(jax.random.uniform(key_cols, (K,), jnp.float32, 0.0, math.log(4.0)))
    return entries * row_scales[:, None] * col_scales[None, :]


def setup_inputs(seed: int = 0) -> dict:
    key_list = jax.random.split(jax.random.key(seed), 4)
    hamiltonian = draw_hamiltonian(jax.random.fold_in(key_list[3], 71), 0)
    start_block = draw_start_block(jax.random.fold_in(key_list[3], 71), 0)
    spectral_bound = jnp.clip(jax.random.uniform(key_list[2], (1,), jnp.float32, 1.25, 1.45), 1.25, 1.45)
    return {"hamiltonian": hamiltonian, "start_block": start_block, "spectral_bound": spectral_bound}


def gram_matrix(vectors):
    return lax.dot_general(vectors.astype(jnp.float32), vectors.astype(jnp.float32), (((0,), (0,)), ((), ())), precision=lax.Precision.HIGHEST, preferred_element_type=jnp.float32)

def right_solve(lower, vectors):
    return lax.linalg.triangular_solve(lower, vectors, left_side=False, lower=True, transpose_a=True)

def orthonormalize(vectors):
    lower_one = jnp.linalg.cholesky(gram_matrix(vectors))
    first_basis = right_solve(lower_one, vectors)
    lower_two = jnp.linalg.cholesky(gram_matrix(first_basis))
    second_basis = right_solve(lower_two, first_basis)
    triangle = jnp.dot(lower_two.T, lower_one.T, precision=lax.Precision.HIGHEST)
    return (second_basis, triangle)

def reference(hamiltonian, start_block, spectral_bound):
    inverse_bound = 1.0 / spectral_bound[0]
    previous = start_block
    current = inverse_bound * jnp.dot(hamiltonian.astype(jnp.float32), previous.astype(jnp.bfloat16).astype(jnp.float32), preferred_element_type=jnp.float32)
    for step in range(1, DEG):
        product = jnp.dot(hamiltonian.astype(jnp.float32), current.astype(jnp.bfloat16).astype(jnp.float32), preferred_element_type=jnp.float32)
        following = 2.0 * inverse_bound * product - previous
        previous = current
        current = following
    second_basis, triangle = orthonormalize(current)
    root = math.sqrt(N)
    return (second_basis * root, triangle / root)
```

```python
import math

import jax
import jax.numpy as jnp
from jax import lax
from jax.sharding import PartitionSpec as P

N = 32768
K = 128
HIGHEST = lax.Precision.HIGHEST
PLANE = ("x", "y")


def contract_rows(left, right, **kwargs):
    return lax.dot_general(
        left, right, (((0,), (0,)), ((), ())), preferred_element_type=jnp.float32, **kwargs
    )


def scatter_sum(parts, axes):
    return jnp.sum(lax.all_to_all(parts, axes, 0, 0, tiled=True).astype(jnp.float32), axis=0)


def gather(block, axes, count):
    copies = jnp.broadcast_to(block[None], (count, *block.shape))
    return lax.all_to_all(copies, axes, 0, 0, tiled=True)


def swap_core(block):
    return lax.ppermute(block, "core", ((0, 1), (1, 0)))


def body(hamiltonian, start_block, spectral_bound):
    inverse_bound = 1.0 / spectral_bound[0]
    block_rows, block_cols = hamiltonian.shape
    row_count = lax.axis_size("row")
    plane_count = lax.axis_size("x") * lax.axis_size("y")
    core = lax.axis_index("core")
    plane = lax.axis_index("x") * lax.axis_size("y") + lax.axis_index("y")
    half = block_rows // 2
    share = half // plane_count
    col_share = block_cols // row_count
    first_row = core * half + plane * share

    def step_even(vectors):
        parts = contract_rows(hamiltonian, vectors).astype(jnp.bfloat16)
        return scatter_sum(parts.reshape(row_count, col_share, K), "row")

    def gather_even(slice_):
        return gather(slice_.astype(jnp.bfloat16), "row", row_count).reshape(block_cols, K)

    def step_odd(vectors):
        part = jnp.dot(hamiltonian, vectors, preferred_element_type=jnp.float32)
        other = lax.dynamic_slice_in_dim(part, (1 - core) * half, half, 0)
        mine = lax.dynamic_slice_in_dim(part, core * half, half, 0)
        pair = mine + swap_core(other.astype(jnp.bfloat16)).astype(jnp.float32)
        return scatter_sum(pair.astype(jnp.bfloat16).reshape(plane_count, share, K), PLANE)

    def gather_odd(slice_):
        mine = gather(slice_, PLANE, plane_count).reshape(half, K)
        other = swap_core(mine)
        whole = jnp.zeros((block_rows, K), slice_.dtype)
        whole = lax.dynamic_update_slice_in_dim(whole, mine, core * half, 0)
        return lax.dynamic_update_slice_in_dim(whole, other, (1 - core) * half, 0)

    def sum_rows(matrix):
        return jnp.sum(gather(matrix, "row", row_count), axis=0)

    def right_solve(lower, vectors):
        return lax.linalg.triangular_solve(
            lower, vectors, left_side=False, lower=True, transpose_a=True
        )

    zeroth = lax.dynamic_slice_in_dim(start_block, first_row, share, 0)
    first = inverse_bound * step_even(start_block.astype(jnp.bfloat16))
    second = 2.0 * inverse_bound * step_odd(gather_even(first)) - zeroth
    third = 2.0 * inverse_bound * step_even(gather_odd(second.astype(jnp.bfloat16))) - first
    fourth = 2.0 * inverse_bound * step_odd(gather_even(third)) - second
    filtered = gather_odd(fourth)

    root = math.sqrt(N)
    lower_one = jnp.linalg.cholesky(sum_rows(contract_rows(filtered, filtered, precision=HIGHEST)))
    first_basis = right_solve(lower_one, filtered)
    lower_two = jnp.linalg.cholesky(
        sum_rows(contract_rows(first_basis, first_basis, precision=HIGHEST))
    )
    out_rows = block_rows // (2 * plane_count)
    out_first = (plane * 2 + core) * out_rows
    own = lax.dynamic_slice_in_dim(first_basis, out_first, out_rows, 0)
    basis = right_solve(lower_two, own) * root
    triangle = jnp.dot(lower_two.T, lower_one.T, precision=HIGHEST)
    return (basis, triangle / root)


def solution(mesh):
    rows = mesh.shape["row"]
    torus = jax.sharding.Mesh(mesh.devices.reshape(rows, 4, 4, 2), ("row", "x", "y", "core"))
    col = ("x", "y", "core")
    in_specs = (P("row", col), P("row", None), P())
    out_specs = (P(("row", *col), None), P())
    return jax.shard_map(
        body, mesh=torus, in_specs=in_specs, out_specs=out_specs, check_vma=False
    )
```

```python
import math

import jax
import jax.numpy as jnp
from jax import lax
from jax.experimental import pallas as pl
from jax.experimental.pallas import tpu as pltpu
from jax.sharding import PartitionSpec as P

N = 32768
K = 128
HALF = K // 2
PACK = HALF + 8
PANEL = 8
HIGHEST = lax.Precision.HIGHEST
PLANE = ("x", "y")


def f32_shape(*shape):
    return jax.ShapeDtypeStruct(shape, jnp.float32)


def gram_of(block):
    return lax.dot_general(
        block, block, (((0,), (0,)), ((), ())), precision=HIGHEST, preferred_element_type=jnp.float32
    )


def times_transposed(block, matrix):
    return lax.dot_general(
        block, matrix, (((1,), (1,)), ((), ())), precision=HIGHEST, preferred_element_type=jnp.float32
    )


def factor(gram, upper_ref, inverse_ref):
    count = K // PANEL
    lane = lax.broadcasted_iota(jnp.int32, (PANEL, K), 1)
    sub = lax.broadcasted_iota(jnp.int32, (PANEL, K), 0)
    left = [gram[i * PANEL : (i + 1) * PANEL, :] for i in range(count)]
    right = [jnp.where(lane == sub + i * PANEL, 1.0, 0.0).astype(jnp.float32) for i in range(count)]
    for b in range(count):
        base = b * PANEL
        cols = [
            [
                jnp.broadcast_to(left[i][:, base + k : base + k + 1], (PANEL, K))
                for i in range(b, count)
            ]
            for k in range(PANEL)
        ]
        for k in range(PANEL):
            j = base + k
            root = lax.rsqrt(cols[k][0][k : k + 1, :])
            left_row = left[b][k : k + 1, :] * root
            right_row = right[b][k : k + 1, :] * root
            upper_ref[j : j + 1, :] = jnp.where(lane[:1] >= j, left_row, 0.0)
            inverse_ref[j : j + 1, :] = right_row
            left_row = left_row * root
            right_row = right_row * root
            heads = [cols[m][0][k : k + 1, :] * (root * root) for m in range(k + 1, PANEL)]
            for i in range(b, count):
                col = cols[k][i - b]
                if i == b:
                    if k == PANEL - 1:
                        continue
                    col = jnp.where(sub > k, col, 0.0)
                for m, head in zip(range(k + 1, PANEL), heads):
                    cols[m][i - b] = cols[m][i - b] - col * head
                left[i] = left[i] - col * left_row
                right[i] = right[i] - col * right_row


def grids():
    shape = (HALF, K)
    return lax.broadcasted_iota(jnp.int32, shape, 0), lax.broadcasted_iota(jnp.int32, shape, 1)


def pack(gram, out_ref):
    top, bottom = gram[:HALF], gram[HALF:]
    row, lane = grids()
    triangles = jnp.where(lane >= row, top, pltpu.roll(bottom, HALF, 1))
    diagonal = jnp.sum(jnp.where(lane == row + HALF, bottom, 0.0), axis=0, keepdims=True)
    for i in range(out_ref.shape[0]):
        out_ref[i, :HALF] = triangles
        out_ref[i, HALF:] = jnp.broadcast_to(diagonal, (PACK - HALF, K))


def unpack_sum(parts_ref):
    packed = parts_ref[0]
    for i in range(1, parts_ref.shape[0]):
        packed = packed + parts_ref[i]
    row, lane = grids()
    triangles, diagonal = packed[:HALF], packed[HALF : HALF + 1]
    last = pltpu.roll(jnp.where(lane < row, triangles, 0.0), HALF, 1)
    strict = jnp.concatenate([jnp.where(lane > row, triangles, 0.0), last], axis=0)
    middle = jnp.concatenate(
        [jnp.where(lane == row, triangles, 0.0), jnp.where(lane == row + HALF, diagonal, 0.0)], axis=0
    )
    return strict + strict.T + middle


def first_gram_kernel(even_ref, odd_ref, out_ref):
    pack(gram_of(even_ref[...]) + gram_of(odd_ref[...]), out_ref)


def second_gram_kernel(parts_ref, even_ref, odd_ref, out_ref, upper_ref, inverse_ref):
    factor(unpack_sum(parts_ref), upper_ref, inverse_ref)
    inverse = inverse_ref[...]
    even = times_transposed(even_ref[...], inverse)
    odd = times_transposed(odd_ref[...], inverse)
    pack(gram_of(even) + gram_of(odd), out_ref)


def last_kernel(
    parts_ref, upper_one_ref, inverse_one_ref, block_ref, basis_ref, triangle_ref, upper_ref, inverse_ref
):
    factor(unpack_sum(parts_ref), upper_ref, inverse_ref)
    root = math.sqrt(N)
    first_basis = times_transposed(block_ref[...], inverse_one_ref[...])
    basis_ref[...] = times_transposed(first_basis, inverse_ref[...]) * root
    product = jnp.dot(
        upper_ref[...], upper_one_ref[...], precision=HIGHEST, preferred_element_type=jnp.float32
    )
    triangle_ref[...] = product / root


def first_gram(count, even, odd):
    return pl.pallas_call(first_gram_kernel, out_shape=f32_shape(count, PACK, K))(even, odd)


def second_gram(parts, even, odd):
    shapes = (f32_shape(*parts.shape), f32_shape(K, K), f32_shape(K, K))
    return pl.pallas_call(second_gram_kernel, out_shape=shapes)(parts, even, odd)


def last_step(parts, upper, inverse, block):
    return pl.pallas_call(
        last_kernel,
        out_shape=(f32_shape(*block.shape), f32_shape(K, K)),
        scratch_shapes=[pltpu.VMEM((K, K), jnp.float32)] * 2,
    )(parts, upper, inverse, block)


def scatter_sum(parts, axes):
    return jnp.sum(lax.all_to_all(parts, axes, 0, 0, tiled=True).astype(jnp.float32), axis=0)


def gather(block, axes, count):
    copies = jnp.broadcast_to(block[None], (count, *block.shape))
    return lax.all_to_all(copies, axes, 0, 0, tiled=True)


def swap_core(block):
    return lax.ppermute(block, "core", ((0, 1), (1, 0)))


def body(hamiltonian, start_block, spectral_bound):
    inverse_bound = 1.0 / spectral_bound[0]
    block_rows, block_cols = hamiltonian.shape
    row_count = lax.axis_size("row")
    plane_count = lax.axis_size("x") * lax.axis_size("y")
    core = lax.axis_index("core")
    plane = lax.axis_index("x") * lax.axis_size("y") + lax.axis_index("y")
    share = block_rows // (2 * plane_count)
    col_share = block_cols // row_count

    def step_even(vectors):
        part = lax.dot_general(
            hamiltonian, vectors, (((0,), (0,)), ((), ())), preferred_element_type=jnp.float32
        )
        return scatter_sum(part.astype(jnp.bfloat16).reshape(row_count, col_share, K), "row")

    def gather_even(slice_):
        return gather(slice_.astype(jnp.bfloat16), "row", row_count).reshape(block_cols, K)

    def step_odd(vectors):
        part = jnp.dot(hamiltonian, vectors, preferred_element_type=jnp.float32)
        part = part.reshape(plane_count, 2, share, K)
        other = lax.dynamic_index_in_dim(part, 1 - core, 1, False)
        mine = lax.dynamic_index_in_dim(part, core, 1, False)
        pair = mine + swap_core(other.astype(jnp.bfloat16)).astype(jnp.float32)
        return scatter_sum(pair.astype(jnp.bfloat16), PLANE)

    def gather_odd(slice_):
        mine = gather(slice_, PLANE, plane_count)
        other = swap_core(mine)
        return (jnp.where(core == 0, mine, other), jnp.where(core == 0, other, mine))

    def interleave(even, odd):
        return jnp.stack([even, odd], axis=1).reshape(block_rows, K)

    zeroth = lax.dynamic_slice_in_dim(start_block, (plane * 2 + core) * share, share, 0)
    first = inverse_bound * step_even(start_block.astype(jnp.bfloat16))
    second = 2.0 * inverse_bound * step_odd(gather_even(first)) - zeroth
    third = 2.0 * inverse_bound * step_even(interleave(*gather_odd(second.astype(jnp.bfloat16)))) - first
    fourth = 2.0 * inverse_bound * step_odd(gather_even(third)) - second

    even, odd = (block.reshape(plane_count * share, K) for block in gather_odd(fourth))

    def exchange(parts):
        return lax.all_to_all(parts, "row", 0, 0, tiled=True)

    parts = exchange(first_gram(row_count, even, odd))
    parts, upper, inverse = second_gram(parts, even, odd)
    return last_step(exchange(parts), upper, inverse, fourth)


def solution(mesh):
    rows = mesh.shape["row"]
    torus = jax.sharding.Mesh(mesh.devices.reshape(rows, 4, 4, 2), ("row", "x", "y", "core"))
    col = ("x", "y", "core")
    in_specs = (P("row", col), P("row", None), P())
    out_specs = (P(("row", *col), None), P())
    return jax.shard_map(
        body, mesh=torus, in_specs=in_specs, out_specs=out_specs, check_vma=False
    )
```

```python
import functools
import math

import jax
import jax.numpy as jnp
from jax import lax
from jax.experimental import pallas as pl
from jax.experimental.pallas import tpu as pltpu
from jax.sharding import PartitionSpec as P

N = 32768
K = 128
HALF = K // 2
PACK = HALF + 8
PANEL = 8
HIGHEST = lax.Precision.HIGHEST
VMEM_LIMIT = 24 * 2**20
COLUMNS = 256
CHUNKS = 4
PLANE = ("x", "y")


def local_call(kernel, out_types, *args, name, out_space=pltpu.VMEM, scratch_shapes=()):
    vmem = pl.BlockSpec(memory_space=pltpu.VMEM)
    return pl.pallas_call(
        kernel,
        in_specs=[vmem] * len(args),
        out_specs=[vmem] * len(out_types),
        out_shape=[out_space(*out_type) for out_type in out_types],
        scratch_shapes=list(scratch_shapes),
        compiler_params=pltpu.CompilerParams(vmem_limit_bytes=VMEM_LIMIT),
        name=name,
    )(*(pltpu.with_memory_space_constraint(arg, pltpu.VMEM) for arg in args))


def gram_of(block):
    return lax.dot_general(
        block, block, (((0,), (0,)), ((), ())), precision=HIGHEST, preferred_element_type=jnp.float32
    )


def times_transposed(block, matrix):
    return lax.dot_general(
        block, matrix, (((1,), (1,)), ((), ())), precision=HIGHEST, preferred_element_type=jnp.float32
    )


def factor(gram, upper_ref, inverse_ref):
    count = K // PANEL
    lane = lax.broadcasted_iota(jnp.int32, (PANEL, K), 1)
    sub = lax.broadcasted_iota(jnp.int32, (PANEL, K), 0)
    left = [gram[i * PANEL : (i + 1) * PANEL, :] for i in range(count)]
    right = [jnp.where(lane == sub + i * PANEL, 1.0, 0.0).astype(jnp.float32) for i in range(count)]
    for b in range(count):
        base = b * PANEL
        cols = [
            [
                jnp.broadcast_to(left[i][:, base + k : base + k + 1], (PANEL, K))
                for i in range(b, count)
            ]
            for k in range(PANEL)
        ]
        for k in range(PANEL):
            j = base + k
            root = lax.rsqrt(cols[k][0][k : k + 1, :])
            left_row = left[b][k : k + 1, :] * root
            right_row = right[b][k : k + 1, :] * root
            upper_ref[j : j + 1, :] = jnp.where(lane[:1] >= j, left_row, 0.0)
            inverse_ref[j : j + 1, :] = right_row
            left_row = left_row * root
            right_row = right_row * root
            heads = [cols[m][0][k : k + 1, :] * (root * root) for m in range(k + 1, PANEL)]
            for i in range(b, count):
                col = cols[k][i - b]
                if i == b:
                    if k == PANEL - 1:
                        continue
                    col = jnp.where(sub > k, col, 0.0)
                for m, head in zip(range(k + 1, PANEL), heads):
                    cols[m][i - b] = cols[m][i - b] - col * head
                left[i] = left[i] - col * left_row
                right[i] = right[i] - col * right_row


def grids():
    shape = (HALF, K)
    return lax.broadcasted_iota(jnp.int32, shape, 0), lax.broadcasted_iota(jnp.int32, shape, 1)


def pack(gram, out_ref):
    top, bottom = gram[:HALF], gram[HALF:]
    row, lane = grids()
    triangles = jnp.where(lane >= row, top, pltpu.roll(bottom, HALF, 1))
    diagonal = jnp.sum(jnp.where(lane == row + HALF, bottom, 0.0), axis=0, keepdims=True)
    for i in range(out_ref.shape[0]):
        out_ref[i, :HALF] = triangles
        out_ref[i, HALF:] = jnp.broadcast_to(diagonal, (PACK - HALF, K))


def sum_copies(parts_ref):
    total = parts_ref[0].astype(jnp.float32)
    for i in range(1, parts_ref.shape[0]):
        total = total + parts_ref[i].astype(jnp.float32)
    return total


def unpack_sum(parts_ref):
    packed = sum_copies(parts_ref)
    row, lane = grids()
    triangles, diagonal = packed[:HALF], packed[HALF : HALF + 1]
    last = pltpu.roll(jnp.where(lane < row, triangles, 0.0), HALF, 1)
    strict = jnp.concatenate([jnp.where(lane > row, triangles, 0.0), last], axis=0)
    middle = jnp.concatenate(
        [jnp.where(lane == row, triangles, 0.0), jnp.where(lane == row + HALF, diagonal, 0.0)], axis=0
    )
    return strict + strict.T + middle


def flat(value):
    return value.reshape(-1, value.shape[-1])


def contract_rows(left, right):
    return lax.dot_general(
        left, right, (((0,), (0,)), ((), ())), preferred_element_type=jnp.float32
    )


def store_row_blocks(product, first, out_ref):
    rows = out_ref.shape[1]
    for i in range(product.shape[1] // rows):
        block = product[:, i * rows : (i + 1) * rows]
        out_ref[first + i] = block.T.astype(out_ref.dtype)


def start_kernel(matrix_ref, start_ref, out_ref, own_ref):
    plane = lax.axis_index("x") * lax.axis_size("y") + lax.axis_index("y")
    own_ref[...] = start_ref[plane, lax.axis_index("core")]
    vectors = start_ref[...].astype(jnp.bfloat16).reshape(-1, K)
    for i in range(matrix_ref.shape[-1] // COLUMNS):
        piece = matrix_ref[:, :, :, i * COLUMNS : (i + 1) * COLUMNS].reshape(-1, COLUMNS)
        store_row_blocks(contract_rows(vectors, piece), i * COLUMNS // out_ref.shape[1], out_ref)


def even_kernel(matrix_ref, mine_ref, other_ref, out_ref):
    core = lax.axis_index("core")
    mine, other = flat(mine_ref[...]), flat(other_ref[...])
    for i in range(matrix_ref.shape[-1] // COLUMNS):
        lanes = slice(i * COLUMNS, (i + 1) * COLUMNS)
        product = contract_rows(mine, flat(matrix_ref[:, core, :, lanes]))
        product = product + contract_rows(other, flat(matrix_ref[:, 1 - core, :, lanes]))
        store_row_blocks(product, i * COLUMNS // out_ref.shape[1], out_ref)


def odd_kernel(offset, matrix_ref, vectors_ref, out_ref):
    core = lax.axis_index("core")
    which = core if offset == 0 else 1 - core
    vectors = flat(vectors_ref[...])
    for i in range(0, out_ref.shape[0], CHUNKS):
        rows = flat(matrix_ref[i : i + CHUNKS, which])
        product = jnp.dot(rows, vectors, preferred_element_type=jnp.float32)
        out_ref[i : i + CHUNKS] = product.reshape(CHUNKS, -1, K).astype(out_ref.dtype)


def pair_kernel(mine_ref, received_ref, out_ref):
    out_ref[...] = (mine_ref[...] + received_ref[...].astype(jnp.float32)).astype(out_ref.dtype)


def first_share_kernel(scale_ref, parts_ref, share_ref, copies_ref):
    total = sum_copies(parts_ref) * scale_ref[:1]
    share_ref[...] = total
    copies_ref[...] = jnp.broadcast_to(total.astype(copies_ref.dtype)[None], copies_ref.shape)


def next_share_kernel(scale_ref, parts_ref, previous_ref, share_ref, copies_ref):
    total = 2.0 * scale_ref[:1] * sum_copies(parts_ref) - previous_ref[...]
    share_ref[...] = total
    copies_ref[...] = jnp.broadcast_to(total.astype(copies_ref.dtype)[None], copies_ref.shape)


def first_gram_kernel(mine_ref, other_ref, out_ref):
    pack(gram_of(flat(mine_ref[...])) + gram_of(flat(other_ref[...])), out_ref)


def second_gram_kernel(parts_ref, mine_ref, other_ref, out_ref, upper_ref, inverse_ref):
    factor(unpack_sum(parts_ref), upper_ref, inverse_ref)
    inverse = inverse_ref[...]
    mine = times_transposed(flat(mine_ref[...]), inverse)
    other = times_transposed(flat(other_ref[...]), inverse)
    pack(gram_of(mine) + gram_of(other), out_ref)


def last_kernel(
    parts_ref, upper_one_ref, inverse_one_ref, block_ref, basis_ref, triangle_ref, upper_ref, inverse_ref
):
    factor(unpack_sum(parts_ref), upper_ref, inverse_ref)
    root = math.sqrt(N)
    first_basis = times_transposed(block_ref[...], inverse_one_ref[...])
    basis_ref[...] = times_transposed(first_basis, inverse_ref[...]) * root
    product = jnp.dot(
        upper_ref[...], upper_one_ref[...], precision=HIGHEST, preferred_element_type=jnp.float32
    )
    triangle_ref[...] = product / root


def swap_core(block):
    return lax.ppermute(block, "core", ((0, 1), (1, 0)))


def exchange(blocks, axes):
    return lax.all_to_all(blocks, axes, 0, 0, tiled=True)


def body(hamiltonian, start_block, spectral_bound):
    f32, bf16 = jnp.float32, jnp.bfloat16
    block_rows, block_cols = hamiltonian.shape
    row_count = lax.axis_size("row")
    plane_count = lax.axis_size("x") * lax.axis_size("y")
    share = block_rows // (2 * plane_count)
    col_share = block_cols // row_count
    scale = jnp.broadcast_to(1.0 / spectral_bound[0], (8, K))
    matrix = hamiltonian.reshape(plane_count, 2, share, block_cols)
    start = start_block.reshape(plane_count, 2, share, K)
    half = (plane_count, share, K)
    columns = (row_count, col_share, K)

    def odd_parts(vectors):
        kernels = [functools.partial(odd_kernel, offset) for offset in (0, 1)]
        (other,) = local_call(kernels[1], [(half, bf16)], matrix, vectors, name="odd_other")
        received = swap_core(other)
        (mine,) = local_call(kernels[0], [(half, f32)], matrix, vectors, name="odd_mine")
        (pair,) = local_call(pair_kernel, [(half, bf16)], mine, received, name="pair")
        return exchange(pair, PLANE)

    def next_share(parts, previous, dtype):
        types = [(previous.shape, f32), (parts.shape, dtype)]
        return local_call(next_share_kernel, types, scale, parts, previous, name="next_share")

    parts, zeroth = local_call(
        start_kernel, [(columns, bf16), ((share, K), f32)], matrix, start, name="start"
    )
    first, copies = local_call(
        first_share_kernel, [((col_share, K), f32), (columns, bf16)], scale, exchange(parts, "row"),
        name="first_share",
    )
    second, copies = next_share(odd_parts(exchange(copies, "row")), zeroth, bf16)
    mine = exchange(copies, PLANE)
    (parts,) = local_call(
        even_kernel, [(columns, bf16)], matrix, mine, swap_core(mine), name="even"
    )
    third, copies = next_share(exchange(parts, "row"), first, bf16)
    fourth, copies = next_share(odd_parts(exchange(copies, "row")), second, f32)

    mine = exchange(copies, PLANE)
    other = swap_core(mine)
    packed = ((row_count, PACK, K), f32)
    square = ((K, K), f32)
    (parts,) = local_call(first_gram_kernel, [packed], mine, other, name="first_gram")
    parts, upper, inverse = local_call(
        second_gram_kernel, [packed, square, square], exchange(parts, "row"), mine, other,
        name="second_gram",
    )
    return local_call(
        last_kernel, [((share, K), f32), square], exchange(parts, "row"), upper, inverse, fourth,
        name="last", out_space=jax.ShapeDtypeStruct, scratch_shapes=[pltpu.VMEM((K, K), f32)] * 2,
    )


def solution(mesh):
    rows = mesh.shape["row"]
    torus = jax.sharding.Mesh(mesh.devices.reshape(rows, 4, 4, 2), ("row", "x", "y", "core"))
    col = ("x", "y", "core")
    in_specs = (P("row", col), P("row", None), P())
    out_specs = (P(("row", *col), None), P())
    return jax.shard_map(
        body, mesh=torus, in_specs=in_specs, out_specs=out_specs, check_vma=False
    )
```

```python
import functools
import math

import jax
import jax.numpy as jnp
from jax import lax
from jax.experimental import pallas as pl
from jax.experimental.pallas import tpu as pltpu
from jax.sharding import PartitionSpec as P

N = 32768
K = 128
HALF = K // 2
PACK = HALF + 8
PANEL = 8
HIGHEST = lax.Precision.HIGHEST
VMEM_LIMIT = 24 * 2**20
COLUMNS = 256
CHUNKS = 4
PLANES = 2
PLANE = ("x", "y")


def local_call(
    kernel, out_types, *args, name, in_space=pltpu.VMEM, out_space=pltpu.VMEM, scratch_shapes=()
):
    vmem = pl.BlockSpec(memory_space=pltpu.VMEM)
    return pl.pallas_call(
        kernel,
        in_specs=[pl.BlockSpec(memory_space=in_space)] * len(args),
        out_specs=[vmem] * len(out_types),
        out_shape=[out_space(*out_type) for out_type in out_types],
        scratch_shapes=list(scratch_shapes),
        compiler_params=pltpu.CompilerParams(vmem_limit_bytes=VMEM_LIMIT),
        name=name,
    )(*(pltpu.with_memory_space_constraint(arg, in_space) for arg in args))


def gram_of(block):
    return lax.dot_general(
        block, block, (((0,), (0,)), ((), ())), precision=HIGHEST, preferred_element_type=jnp.float32
    )


def times_transposed(block, matrix):
    return lax.dot_general(
        block, matrix, (((1,), (1,)), ((), ())), precision=HIGHEST, preferred_element_type=jnp.float32
    )


def factor(gram, upper_ref, inverse_ref):
    count = K // PANEL
    lane = lax.broadcasted_iota(jnp.int32, (PANEL, K), 1)
    sub = lax.broadcasted_iota(jnp.int32, (PANEL, K), 0)
    left = [gram[i * PANEL : (i + 1) * PANEL, :] for i in range(count)]
    right = [jnp.where(lane == sub + i * PANEL, 1.0, 0.0).astype(jnp.float32) for i in range(count)]
    for b in range(count):
        base = b * PANEL
        cols = [
            [
                jnp.broadcast_to(left[i][:, base + k : base + k + 1], (PANEL, K))
                for i in range(b, count)
            ]
            for k in range(PANEL)
        ]
        for k in range(PANEL):
            j = base + k
            root = lax.rsqrt(cols[k][0][k : k + 1, :])
            left_row = left[b][k : k + 1, :] * root
            right_row = right[b][k : k + 1, :] * root
            upper_ref[j : j + 1, :] = jnp.where(lane[:1] >= j, left_row, 0.0)
            inverse_ref[j : j + 1, :] = right_row
            left_row = left_row * root
            right_row = right_row * root
            heads = [cols[m][0][k : k + 1, :] * (root * root) for m in range(k + 1, PANEL)]
            for i in range(b, count):
                col = cols[k][i - b]
                if i == b:
                    if k == PANEL - 1:
                        continue
                    col = jnp.where(sub > k, col, 0.0)
                for m, head in zip(range(k + 1, PANEL), heads):
                    cols[m][i - b] = cols[m][i - b] - col * head
                left[i] = left[i] - col * left_row
                right[i] = right[i] - col * right_row


def grids():
    shape = (HALF, K)
    return lax.broadcasted_iota(jnp.int32, shape, 0), lax.broadcasted_iota(jnp.int32, shape, 1)


def pack(gram, out_ref):
    top, bottom = gram[:HALF], gram[HALF:]
    row, lane = grids()
    triangles = jnp.where(lane >= row, top, pltpu.roll(bottom, HALF, 1))
    diagonal = jnp.sum(jnp.where(lane == row + HALF, bottom, 0.0), axis=0, keepdims=True)
    for i in range(out_ref.shape[0]):
        out_ref[i, :HALF] = triangles
        out_ref[i, HALF:] = jnp.broadcast_to(diagonal, (PACK - HALF, K))


def sum_copies(parts_ref):
    total = parts_ref[0].astype(jnp.float32)
    for i in range(1, parts_ref.shape[0]):
        total = total + parts_ref[i].astype(jnp.float32)
    return total


def unpack_sum(parts_ref):
    packed = sum_copies(parts_ref)
    row, lane = grids()
    triangles, diagonal = packed[:HALF], packed[HALF : HALF + 1]
    last = pltpu.roll(jnp.where(lane < row, triangles, 0.0), HALF, 1)
    strict = jnp.concatenate([jnp.where(lane > row, triangles, 0.0), last], axis=0)
    middle = jnp.concatenate(
        [jnp.where(lane == row, triangles, 0.0), jnp.where(lane == row + HALF, diagonal, 0.0)], axis=0
    )
    return strict + strict.T + middle


def flat(value):
    return value.reshape(-1, value.shape[-1])


def contract_rows(left, right):
    return lax.dot_general(
        left, right, (((0,), (0,)), ((), ())), preferred_element_type=jnp.float32
    )


def store_row_blocks(product, first, out_ref):
    rows = out_ref.shape[1]
    for i in range(product.shape[1] // rows):
        block = product[:, i * rows : (i + 1) * rows]
        out_ref[first + i] = block.T.astype(out_ref.dtype)


def start_kernel(
    matrix_ref, start_ref, out_ref, own_ref, kept_ref, vectors_ref, total_ref, matrix_sems, start_sems
):
    pieces = []
    for i in range(0, matrix_ref.shape[0], PLANES):
        part, n = pl.ds(i, PLANES), i // PLANES
        copies = (
            pltpu.make_async_copy(start_ref.at[part], vectors_ref.at[part], start_sems.at[n]),
            pltpu.make_async_copy(matrix_ref.at[part], kept_ref.at[part], matrix_sems.at[n]),
        )
        for copy in copies:
            copy.start()
        pieces.append(copies)
    for n, copies in enumerate(pieces):
        for copy in copies:
            copy.wait()
        part = slice(n * PLANES, (n + 1) * PLANES)
        vectors = vectors_ref[part].astype(jnp.bfloat16).reshape(-1, K)
        product = contract_rows(vectors, kept_ref[part].reshape(-1, kept_ref.shape[-1]))
        total_ref[...] = product if n == 0 else total_ref[...] + product
    store_row_blocks(total_ref[...], 0, out_ref)
    plane = lax.axis_index("x") * lax.axis_size("y") + lax.axis_index("y")
    own_ref[...] = vectors_ref[plane, lax.axis_index("core")]


def even_kernel(matrix_ref, mine_ref, other_ref, out_ref):
    core = lax.axis_index("core")
    mine, other = flat(mine_ref[...]), flat(other_ref[...])
    for i in range(matrix_ref.shape[-1] // COLUMNS):
        lanes = slice(i * COLUMNS, (i + 1) * COLUMNS)
        product = contract_rows(mine, flat(matrix_ref[:, core, :, lanes]))
        product = product + contract_rows(other, flat(matrix_ref[:, 1 - core, :, lanes]))
        store_row_blocks(product, i * COLUMNS // out_ref.shape[1], out_ref)


def odd_kernel(offset, matrix_ref, vectors_ref, out_ref):
    core = lax.axis_index("core")
    which = core if offset == 0 else 1 - core
    vectors = flat(vectors_ref[...])
    for i in range(0, out_ref.shape[0], CHUNKS):
        rows = flat(matrix_ref[i : i + CHUNKS, which])
        product = jnp.dot(rows, vectors, preferred_element_type=jnp.float32)
        out_ref[i : i + CHUNKS] = product.reshape(CHUNKS, -1, K).astype(out_ref.dtype)


def pair_kernel(mine_ref, received_ref, out_ref):
    out_ref[...] = (mine_ref[...] + received_ref[...].astype(jnp.float32)).astype(out_ref.dtype)


def first_share_kernel(scale_ref, parts_ref, share_ref, copies_ref):
    total = sum_copies(parts_ref) * scale_ref[:1]
    share_ref[...] = total
    copies_ref[...] = jnp.broadcast_to(total.astype(copies_ref.dtype)[None], copies_ref.shape)


def next_share_kernel(scale_ref, parts_ref, previous_ref, *out_refs):
    total = 2.0 * scale_ref[:1] * sum_copies(parts_ref) - previous_ref[...]
    copies_ref = out_refs[-1]
    copies_ref[...] = jnp.broadcast_to(total.astype(copies_ref.dtype)[None], copies_ref.shape)
    if len(out_refs) == 2:
        out_refs[0][...] = total


def times_inverse(block, inverse):
    total = None
    for _ in range(3):
        term = inverse.astype(jnp.bfloat16)
        inverse = inverse - term.astype(jnp.float32)
        product = lax.dot_general(
            block, term, (((1,), (1,)), ((), ())), preferred_element_type=jnp.float32
        )
        total = product if total is None else total + product
    return total


def first_gram_kernel(mine_ref, other_ref, out_ref):
    mine, other = flat(mine_ref[...]), flat(other_ref[...])
    pack(contract_rows(mine, mine) + contract_rows(other, other), out_ref)


def second_gram_kernel(parts_ref, mine_ref, other_ref, out_ref, upper_ref, inverse_ref):
    factor(unpack_sum(parts_ref), upper_ref, inverse_ref)
    inverse = inverse_ref[...]
    mine = times_inverse(flat(mine_ref[...]), inverse)
    other = times_inverse(flat(other_ref[...]), inverse)
    pack(gram_of(mine) + gram_of(other), out_ref)


def last_kernel(
    parts_ref, upper_one_ref, inverse_one_ref, block_ref, basis_ref, triangle_ref, upper_ref, inverse_ref
):
    factor(unpack_sum(parts_ref), upper_ref, inverse_ref)
    root = math.sqrt(N)
    first_basis = times_inverse(block_ref[0], inverse_one_ref[...])
    basis_ref[...] = times_transposed(first_basis, inverse_ref[...]) * root
    product = jnp.dot(
        upper_ref[...], upper_one_ref[...], precision=HIGHEST, preferred_element_type=jnp.float32
    )
    triangle_ref[...] = product / root


def swap_core(block):
    return lax.ppermute(block, "core", ((0, 1), (1, 0)))


def exchange(blocks, axes):
    return lax.all_to_all(blocks, axes, 0, 0, tiled=True)


def body(hamiltonian, start_block, spectral_bound):
    f32, bf16 = jnp.float32, jnp.bfloat16
    block_rows, block_cols = hamiltonian.shape
    row_count = lax.axis_size("row")
    plane_count = lax.axis_size("x") * lax.axis_size("y")
    share = block_rows // (2 * plane_count)
    col_share = block_cols // row_count
    scale = jnp.broadcast_to(1.0 / spectral_bound[0], (8, K))
    matrix = hamiltonian.reshape(plane_count, 2, share, block_cols)
    start = start_block.reshape(plane_count, 2, share, K)
    half = (plane_count, share, K)
    columns = (row_count, col_share, K)

    def odd_parts(vectors):
        kernels = [functools.partial(odd_kernel, offset) for offset in (0, 1)]
        (other,) = local_call(kernels[1], [(half, bf16)], matrix, vectors, name="odd_other")
        received = swap_core(other)
        (mine,) = local_call(kernels[0], [(half, f32)], matrix, vectors, name="odd_mine")
        (pair,) = local_call(pair_kernel, [(half, bf16)], mine, received, name="pair")
        return exchange(pair, PLANE)

    def next_share(parts, previous, keep):
        types = [(previous.shape, f32)] * keep + [(parts.shape, bf16)]
        return local_call(next_share_kernel, types, scale, parts, previous, name="next_share")

    pieces = plane_count // PLANES
    parts, zeroth, matrix = local_call(
        start_kernel, [(columns, bf16), ((share, K), f32), (matrix.shape, bf16)], matrix, start,
        name="start", in_space=pltpu.HBM, scratch_shapes=[
            pltpu.VMEM(start.shape, f32), pltpu.VMEM((K, block_cols), f32),
            pltpu.SemaphoreType.DMA((pieces,)), pltpu.SemaphoreType.DMA((pieces,)),
        ],
    )
    first, copies = local_call(
        first_share_kernel, [((col_share, K), f32), (columns, bf16)], scale, exchange(parts, "row"),
        name="first_share",
    )
    second, copies = next_share(odd_parts(exchange(copies, "row")), zeroth, True)
    mine = exchange(copies, PLANE)
    (parts,) = local_call(
        even_kernel, [(columns, bf16)], matrix, mine, swap_core(mine), name="even"
    )
    (copies,) = next_share(exchange(parts, "row"), first, False)
    (copies,) = next_share(odd_parts(exchange(copies, "row")), second, False)

    mine = exchange(copies, PLANE)
    other = swap_core(mine)
    packed = ((row_count, PACK, K), f32)
    square = ((K, K), f32)
    (parts,) = local_call(first_gram_kernel, [packed], mine, other, name="first_gram")
    parts, upper, inverse = local_call(
        second_gram_kernel, [packed, square, square], exchange(parts, "row"), mine, other,
        name="second_gram",
    )
    return local_call(
        last_kernel, [((share, K), f32), square], exchange(parts, "row"), upper, inverse, copies,
        name="last", out_space=jax.ShapeDtypeStruct, scratch_shapes=[pltpu.VMEM((K, K), f32)] * 2,
    )


def solution(mesh):
    rows = mesh.shape["row"]
    torus = jax.sharding.Mesh(mesh.devices.reshape(rows, 4, 4, 2), ("row", "x", "y", "core"))
    col = ("x", "y", "core")
    in_specs = (P("row", col), P("row", None), P())
    out_specs = (P(("row", *col), None), P())
    return jax.shard_map(
        body, mesh=torus, in_specs=in_specs, out_specs=out_specs, check_vma=False
    )
```

```python
import functools
import math

import jax
import jax.numpy as jnp
from jax import lax
from jax.experimental import pallas as pl
from jax.experimental.pallas import tpu as pltpu
from jax.sharding import PartitionSpec as P

N = 32768
K = 128
HALF = K // 2
PACK = HALF + 8
PANEL = 8
HIGHEST = lax.Precision.HIGHEST
VMEM_LIMIT = 24 * 2**20
COLUMNS = 256
CHUNKS = 4
PLANES = 2
PLANE = ("x", "y")


def local_call(
    kernel, out_types, *args, name, in_spaces=None, out_space=pltpu.VMEM, scratch_shapes=()
):
    vmem = pl.BlockSpec(memory_space=pltpu.VMEM)
    in_spaces = in_spaces or [pltpu.VMEM] * len(args)
    return pl.pallas_call(
        kernel,
        in_specs=[pl.BlockSpec(memory_space=space) for space in in_spaces],
        out_specs=[vmem] * len(out_types),
        out_shape=[out_space(*out_type) for out_type in out_types],
        scratch_shapes=list(scratch_shapes),
        compiler_params=pltpu.CompilerParams(vmem_limit_bytes=VMEM_LIMIT),
        name=name,
    )(*(pltpu.with_memory_space_constraint(*pair) for pair in zip(args, in_spaces)))


def gram_of(block):
    return lax.dot_general(
        block, block, (((0,), (0,)), ((), ())), precision=HIGHEST, preferred_element_type=jnp.float32
    )


def times_transposed(block, matrix):
    return lax.dot_general(
        block, matrix, (((1,), (1,)), ((), ())), precision=HIGHEST, preferred_element_type=jnp.float32
    )


def factor(gram, upper_ref, inverse_ref):
    count = K // PANEL
    lane = lax.broadcasted_iota(jnp.int32, (PANEL, K), 1)
    sub = lax.broadcasted_iota(jnp.int32, (PANEL, K), 0)
    left = [gram[i * PANEL : (i + 1) * PANEL, :] for i in range(count)]
    right = [jnp.where(lane == sub + i * PANEL, 1.0, 0.0).astype(jnp.float32) for i in range(count)]
    for b in range(count):
        base = b * PANEL
        cols = [
            [
                jnp.broadcast_to(left[i][:, base + k : base + k + 1], (PANEL, K))
                for i in range(b, count)
            ]
            for k in range(PANEL)
        ]
        for k in range(PANEL):
            j = base + k
            root = lax.rsqrt(cols[k][0][k : k + 1, :])
            left_row = left[b][k : k + 1, :] * root
            right_row = right[b][k : k + 1, :] * root
            upper_ref[j : j + 1, :] = jnp.where(lane[:1] >= j, left_row, 0.0)
            inverse_ref[j : j + 1, :] = right_row
            left_row = left_row * root
            right_row = right_row * root
            heads = [cols[m][0][k : k + 1, :] * (root * root) for m in range(k + 1, PANEL)]
            for i in range(b, count):
                col = cols[k][i - b]
                if i == b:
                    if k == PANEL - 1:
                        continue
                    col = jnp.where(sub > k, col, 0.0)
                for m, head in zip(range(k + 1, PANEL), heads):
                    cols[m][i - b] = cols[m][i - b] - col * head
                left[i] = left[i] - col * left_row
                right[i] = right[i] - col * right_row


def grids():
    shape = (HALF, K)
    return lax.broadcasted_iota(jnp.int32, shape, 0), lax.broadcasted_iota(jnp.int32, shape, 1)


def pack(gram, out_ref):
    top, bottom = gram[:HALF], gram[HALF:]
    row, lane = grids()
    triangles = jnp.where(lane >= row, top, pltpu.roll(bottom, HALF, 1))
    diagonal = jnp.sum(jnp.where(lane == row + HALF, bottom, 0.0), axis=0, keepdims=True)
    for i in range(out_ref.shape[0]):
        out_ref[i, :HALF] = triangles
        out_ref[i, HALF:] = jnp.broadcast_to(diagonal, (PACK - HALF, K))


def sum_copies(parts_ref):
    total = parts_ref[0].astype(jnp.float32)
    for i in range(1, parts_ref.shape[0]):
        total = total + parts_ref[i].astype(jnp.float32)
    return total


def unpack_sum(parts_ref):
    packed = sum_copies(parts_ref)
    row, lane = grids()
    triangles, diagonal = packed[:HALF], packed[HALF : HALF + 1]
    last = pltpu.roll(jnp.where(lane < row, triangles, 0.0), HALF, 1)
    strict = jnp.concatenate([jnp.where(lane > row, triangles, 0.0), last], axis=0)
    middle = jnp.concatenate(
        [jnp.where(lane == row, triangles, 0.0), jnp.where(lane == row + HALF, diagonal, 0.0)], axis=0
    )
    return strict + strict.T + middle


def flat(value):
    return value.reshape(-1, value.shape[-1])


def contract_rows(left, right):
    return lax.dot_general(
        left, right, (((0,), (0,)), ((), ())), preferred_element_type=jnp.float32
    )


def store_row_blocks(product, first, out_ref):
    rows = out_ref.shape[1]
    for i in range(product.shape[1] // rows):
        block = product[:, i * rows : (i + 1) * rows]
        out_ref[first + i] = block.T.astype(out_ref.dtype)


def start_kernel(
    matrix_ref, start_ref, bound_ref, out_ref, own_ref, kept_ref, scale_ref,
    vectors_ref, total_ref, matrix_sems, start_sems,
):
    pieces = []
    for i in range(0, matrix_ref.shape[0], PLANES):
        part, n = pl.ds(i, PLANES), i // PLANES
        copies = (
            pltpu.make_async_copy(start_ref.at[part], vectors_ref.at[part], start_sems.at[n]),
            pltpu.make_async_copy(matrix_ref.at[part], kept_ref.at[part], matrix_sems.at[n]),
        )
        for copy in copies:
            copy.start()
        pieces.append(copies)
    scale_ref[...] = 1.0 / jnp.full(scale_ref.shape, bound_ref[0], jnp.float32)
    for n, copies in enumerate(pieces):
        for copy in copies:
            copy.wait()
        part = slice(n * PLANES, (n + 1) * PLANES)
        vectors = vectors_ref[part].astype(jnp.bfloat16).reshape(-1, K)
        product = contract_rows(vectors, kept_ref[part].reshape(-1, kept_ref.shape[-1]))
        total_ref[...] = product if n == 0 else total_ref[...] + product
    store_row_blocks(total_ref[...], 0, out_ref)
    plane = lax.axis_index("x") * lax.axis_size("y") + lax.axis_index("y")
    own_ref[...] = vectors_ref[plane, lax.axis_index("core")]


def even_kernel(matrix_ref, mine_ref, other_ref, out_ref):
    core = lax.axis_index("core")
    mine, other = flat(mine_ref[...]), flat(other_ref[...])
    for i in range(matrix_ref.shape[-1] // COLUMNS):
        lanes = slice(i * COLUMNS, (i + 1) * COLUMNS)
        product = contract_rows(mine, flat(matrix_ref[:, core, :, lanes]))
        product = product + contract_rows(other, flat(matrix_ref[:, 1 - core, :, lanes]))
        store_row_blocks(product, i * COLUMNS // out_ref.shape[1], out_ref)


def odd_kernel(offset, matrix_ref, vectors_ref, out_ref):
    core = lax.axis_index("core")
    which = core if offset == 0 else 1 - core
    vectors = flat(vectors_ref[...])
    for i in range(0, out_ref.shape[0], CHUNKS):
        rows = flat(matrix_ref[i : i + CHUNKS, which])
        product = jnp.dot(rows, vectors, preferred_element_type=jnp.float32)
        out_ref[i : i + CHUNKS] = product.reshape(CHUNKS, -1, K).astype(out_ref.dtype)


def pair_kernel(mine_ref, received_ref, out_ref):
    out_ref[...] = (mine_ref[...] + received_ref[...].astype(jnp.float32)).astype(out_ref.dtype)


def first_share_kernel(scale_ref, parts_ref, share_ref, copies_ref):
    total = sum_copies(parts_ref) * scale_ref[:1]
    share_ref[...] = total
    copies_ref[...] = jnp.broadcast_to(total.astype(copies_ref.dtype)[None], copies_ref.shape)


def next_share_kernel(scale_ref, parts_ref, previous_ref, *out_refs):
    total = 2.0 * scale_ref[:1] * sum_copies(parts_ref) - previous_ref[...]
    copies_ref = out_refs[-1]
    copies_ref[...] = jnp.broadcast_to(total.astype(copies_ref.dtype)[None], copies_ref.shape)
    if len(out_refs) == 2:
        out_refs[0][...] = total


def times_inverse(block, inverse):
    total = None
    for _ in range(3):
        term = inverse.astype(jnp.bfloat16)
        inverse = inverse - term.astype(jnp.float32)
        product = lax.dot_general(
            block, term, (((1,), (1,)), ((), ())), preferred_element_type=jnp.float32
        )
        total = product if total is None else total + product
    return total


def first_gram_kernel(mine_ref, other_ref, out_ref):
    mine, other = flat(mine_ref[...]), flat(other_ref[...])
    pack(contract_rows(mine, mine) + contract_rows(other, other), out_ref)


def second_gram_kernel(parts_ref, mine_ref, other_ref, out_ref, upper_ref, inverse_ref):
    factor(unpack_sum(parts_ref), upper_ref, inverse_ref)
    inverse = inverse_ref[...]
    mine = times_inverse(flat(mine_ref[...]), inverse)
    other = times_inverse(flat(other_ref[...]), inverse)
    pack(gram_of(mine) + gram_of(other), out_ref)


def last_kernel(
    parts_ref, upper_one_ref, inverse_one_ref, block_ref, basis_ref, triangle_ref, upper_ref, inverse_ref
):
    factor(unpack_sum(parts_ref), upper_ref, inverse_ref)
    root = math.sqrt(N)
    first_basis = times_inverse(block_ref[0], inverse_one_ref[...])
    basis_ref[...] = times_transposed(first_basis, inverse_ref[...]) * root
    product = jnp.dot(
        upper_ref[...], upper_one_ref[...], precision=HIGHEST, preferred_element_type=jnp.float32
    )
    triangle_ref[...] = product / root


def swap_core(block):
    return lax.ppermute(block, "core", ((0, 1), (1, 0)))


def exchange(blocks, axes):
    return lax.all_to_all(blocks, axes, 0, 0, tiled=True)


def body(hamiltonian, start_block, spectral_bound):
    f32, bf16 = jnp.float32, jnp.bfloat16
    block_rows, block_cols = hamiltonian.shape
    row_count = lax.axis_size("row")
    plane_count = lax.axis_size("x") * lax.axis_size("y")
    share = block_rows // (2 * plane_count)
    col_share = block_cols // row_count
    matrix = hamiltonian.reshape(plane_count, 2, share, block_cols)
    start = start_block.reshape(plane_count, 2, share, K)
    half = (plane_count, share, K)
    columns = (row_count, col_share, K)

    def odd_parts(vectors):
        kernels = [functools.partial(odd_kernel, offset) for offset in (0, 1)]
        (other,) = local_call(kernels[1], [(half, bf16)], matrix, vectors, name="odd_other")
        received = swap_core(other)
        (mine,) = local_call(kernels[0], [(half, f32)], matrix, vectors, name="odd_mine")
        (pair,) = local_call(pair_kernel, [(half, bf16)], mine, received, name="pair")
        return exchange(pair, PLANE)

    def next_share(parts, previous, keep):
        types = [(previous.shape, f32)] * keep + [(parts.shape, bf16)]
        return local_call(next_share_kernel, types, scale, parts, previous, name="next_share")

    pieces = plane_count // PLANES
    parts, zeroth, matrix, scale = local_call(
        start_kernel, [(columns, bf16), ((share, K), f32), (matrix.shape, bf16), ((8, K), f32)],
        matrix, start, spectral_bound, name="start", in_spaces=[pltpu.HBM, pltpu.HBM, pltpu.SMEM],
        scratch_shapes=[
            pltpu.VMEM(start.shape, f32), pltpu.VMEM((K, block_cols), f32),
            pltpu.SemaphoreType.DMA((pieces,)), pltpu.SemaphoreType.DMA((pieces,)),
        ],
    )
    first, copies = local_call(
        first_share_kernel, [((col_share, K), f32), (columns, bf16)], scale, exchange(parts, "row"),
        name="first_share",
    )
    second, copies = next_share(odd_parts(exchange(copies, "row")), zeroth, True)
    mine = exchange(copies, PLANE)
    (parts,) = local_call(
        even_kernel, [(columns, bf16)], matrix, mine, swap_core(mine), name="even"
    )
    (copies,) = next_share(exchange(parts, "row"), first, False)
    (copies,) = next_share(odd_parts(exchange(copies, "row")), second, False)

    mine = exchange(copies, PLANE)
    other = swap_core(mine)
    packed = ((row_count, PACK, K), f32)
    square = ((K, K), f32)
    (parts,) = local_call(first_gram_kernel, [packed], mine, other, name="first_gram")
    parts, upper, inverse = local_call(
        second_gram_kernel, [packed, square, square], exchange(parts, "row"), mine, other,
        name="second_gram",
    )
    return local_call(
        last_kernel, [((share, K), f32), square], exchange(parts, "row"), upper, inverse, copies,
        name="last", out_space=jax.ShapeDtypeStruct, scratch_shapes=[pltpu.VMEM((K, K), f32)] * 2,
    )


def solution(mesh):
    rows = mesh.shape["row"]
    torus = jax.sharding.Mesh(mesh.devices.reshape(rows, 4, 4, 2), ("row", "x", "y", "core"))
    col = ("x", "y", "core")
    in_specs = (P("row", col), P("row", None), P())
    out_specs = (P(("row", *col), None), P())
    return jax.shard_map(
        body, mesh=torus, in_specs=in_specs, out_specs=out_specs, check_vma=False
    )
```

```python
import functools
import math

import jax
import jax.numpy as jnp
from jax import lax
from jax.experimental import pallas as pl
from jax.experimental.pallas import tpu as pltpu
from jax.sharding import PartitionSpec as P

N = 32768
K = 128
HALF = K // 2
PACK = HALF + 8
PANEL = 8
HIGHEST = lax.Precision.HIGHEST
VMEM_LIMIT = 24 * 2**20
COLUMNS = 256
CHUNKS = 4
PLANES = 2
PLANE = ("x", "y")


def local_call(
    kernel, out_types, *args, name, in_spaces=None, out_space=pltpu.VMEM, scratch_shapes=()
):
    vmem = pl.BlockSpec(memory_space=pltpu.VMEM)
    in_spaces = in_spaces or [pltpu.VMEM] * len(args)
    return pl.pallas_call(
        kernel,
        in_specs=[pl.BlockSpec(memory_space=space) for space in in_spaces],
        out_specs=[vmem] * len(out_types),
        out_shape=[out_space(*out_type) for out_type in out_types],
        scratch_shapes=list(scratch_shapes),
        compiler_params=pltpu.CompilerParams(vmem_limit_bytes=VMEM_LIMIT),
        name=name,
    )(*(pltpu.with_memory_space_constraint(*pair) for pair in zip(args, in_spaces)))


def gram_of(block):
    return lax.dot_general(
        block, block, (((0,), (0,)), ((), ())), precision=HIGHEST, preferred_element_type=jnp.float32
    )


def times_transposed(block, matrix):
    return lax.dot_general(
        block, matrix, (((1,), (1,)), ((), ())), precision=HIGHEST, preferred_element_type=jnp.float32
    )


def factor(gram, upper_ref, inverse_ref):
    count = K // PANEL
    lane = lax.broadcasted_iota(jnp.int32, (PANEL, K), 1)
    sub = lax.broadcasted_iota(jnp.int32, (PANEL, K), 0)
    left = [gram[i * PANEL : (i + 1) * PANEL, :] for i in range(count)]
    right = [jnp.where(lane == sub + i * PANEL, 1.0, 0.0).astype(jnp.float32) for i in range(count)]
    for b in range(count):
        base = b * PANEL
        cols = [
            [
                jnp.broadcast_to(left[i][:, base + k : base + k + 1], (PANEL, K))
                for i in range(b, count)
            ]
            for k in range(PANEL)
        ]
        for k in range(PANEL):
            j = base + k
            root = lax.rsqrt(cols[k][0][k : k + 1, :])
            left_row = left[b][k : k + 1, :] * root
            right_row = right[b][k : k + 1, :] * root
            upper_ref[j : j + 1, :] = jnp.where(lane[:1] >= j, left_row, 0.0)
            inverse_ref[j : j + 1, :] = right_row
            left_row = left_row * root
            right_row = right_row * root
            heads = [cols[m][0][k : k + 1, :] * (root * root) for m in range(k + 1, PANEL)]
            for i in range(b, count):
                col = cols[k][i - b]
                if i == b:
                    if k == PANEL - 1:
                        continue
                    col = jnp.where(sub > k, col, 0.0)
                for m, head in zip(range(k + 1, PANEL), heads):
                    cols[m][i - b] = cols[m][i - b] - col * head
                left[i] = left[i] - col * left_row
                right[i] = right[i] - col * right_row


def grids():
    shape = (HALF, K)
    return lax.broadcasted_iota(jnp.int32, shape, 0), lax.broadcasted_iota(jnp.int32, shape, 1)


def pack(gram, out_ref):
    top, bottom = gram[:HALF], gram[HALF:]
    row, lane = grids()
    triangles = jnp.where(lane >= row, top, pltpu.roll(bottom, HALF, 1))
    diagonal = jnp.sum(jnp.where(lane == row + HALF, bottom, 0.0), axis=0, keepdims=True)
    for i in range(out_ref.shape[0]):
        out_ref[i, :HALF] = triangles
        out_ref[i, HALF:] = jnp.broadcast_to(diagonal, (PACK - HALF, K))


def sum_copies(parts_ref):
    total = parts_ref[0].astype(jnp.float32)
    for i in range(1, parts_ref.shape[0]):
        total = total + parts_ref[i].astype(jnp.float32)
    return total


def unpack_sum(parts_ref):
    packed = sum_copies(parts_ref)
    row, lane = grids()
    triangles, diagonal = packed[:HALF], packed[HALF : HALF + 1]
    last = pltpu.roll(jnp.where(lane < row, triangles, 0.0), HALF, 1)
    strict = jnp.concatenate([jnp.where(lane > row, triangles, 0.0), last], axis=0)
    middle = jnp.concatenate(
        [jnp.where(lane == row, triangles, 0.0), jnp.where(lane == row + HALF, diagonal, 0.0)], axis=0
    )
    return strict + strict.T + middle


def flat(value):
    return value.reshape(-1, value.shape[-1])


def contract_rows(left, right):
    return lax.dot_general(
        left, right, (((0,), (0,)), ((), ())), preferred_element_type=jnp.float32
    )


def store_row_blocks(product, first, out_ref):
    rows = out_ref.shape[1]
    for i in range(product.shape[1] // rows):
        block = product[:, i * rows : (i + 1) * rows]
        out_ref[first + i] = block.T.astype(out_ref.dtype)


def pair_half():
    row = lax.axis_index("row")
    return lax.rem(row + lax.div(row, 4), 2)


def start_kernel(
    matrix_ref, start_ref, bound_ref, other_ref, mine_ref, own_ref, kept_ref, scale_ref,
    vectors_ref, total_ref, matrix_sems, start_sems,
):
    pieces = []
    for i in range(0, matrix_ref.shape[0], PLANES):
        part, n = pl.ds(i, PLANES), i // PLANES
        copies = (
            pltpu.make_async_copy(start_ref.at[part], vectors_ref.at[part], start_sems.at[n]),
            pltpu.make_async_copy(matrix_ref.at[part], kept_ref.at[part], matrix_sems.at[n]),
        )
        for copy in copies:
            copy.start()
        pieces.append(copies)
    scale_ref[...] = 1.0 / jnp.full(scale_ref.shape, bound_ref[0], jnp.float32)
    for n, copies in enumerate(pieces):
        for copy in copies:
            copy.wait()
        part = slice(n * PLANES, (n + 1) * PLANES)
        vectors = vectors_ref[part].astype(jnp.bfloat16).reshape(-1, K)
        product = contract_rows(vectors, kept_ref[part].reshape(-1, kept_ref.shape[-1]))
        total_ref[...] = product if n == 0 else total_ref[...] + product
    half = total_ref.shape[1] // 2
    for own in (0, 1):

        @pl.when(pair_half() == own)
        def _():
            store_row_blocks(total_ref[:, own * half : (own + 1) * half], 0, mine_ref)
            store_row_blocks(total_ref[:, (1 - own) * half : (2 - own) * half], 0, other_ref)

    plane = lax.axis_index("x") * lax.axis_size("y") + lax.axis_index("y")
    own_ref[...] = vectors_ref[plane, lax.axis_index("core")]


def even_kernel(offset, matrix_ref, mine_ref, other_ref, out_ref):
    core = lax.axis_index("core")
    mine, other = flat(mine_ref[...]), flat(other_ref[...])
    half = matrix_ref.shape[-1] // 2
    for own in (0, 1):

        @pl.when(pair_half() == own)
        def _():
            base = (own ^ offset) * half
            for i in range(0, half, COLUMNS):
                lanes = slice(base + i, base + i + COLUMNS)
                product = contract_rows(mine, flat(matrix_ref[:, core, :, lanes]))
                product = product + contract_rows(other, flat(matrix_ref[:, 1 - core, :, lanes]))
                store_row_blocks(product, i // out_ref.shape[1], out_ref)


def odd_half(offset, column_offset, matrix_ref, vectors_ref, base_ref, out_ref):
    core = lax.axis_index("core")
    which = core if offset == 0 else 1 - core
    vectors = flat(vectors_ref[...])
    half = matrix_ref.shape[-1] // 2
    for own in (0, 1):

        @pl.when(pair_half() == own)
        def _():
            base = (own ^ column_offset) * half
            for i in range(0, out_ref.shape[0], CHUNKS):
                rows = flat(matrix_ref[i : i + CHUNKS, which, :, base : base + half])
                product = jnp.dot(rows, vectors, preferred_element_type=jnp.float32)
                product = product.reshape(CHUNKS, -1, K)
                if base_ref is not None:
                    product = product + base_ref[i : i + CHUNKS]
                out_ref[i : i + CHUNKS] = product.astype(out_ref.dtype)


def odd_first_kernel(matrix_ref, vectors_ref, other_ref, mine_ref):
    odd_half(1, 0, matrix_ref, vectors_ref, None, other_ref)
    odd_half(0, 0, matrix_ref, vectors_ref, None, mine_ref)


def odd_last_kernel(offset, matrix_ref, vectors_ref, base_ref, out_ref):
    odd_half(offset, 1, matrix_ref, vectors_ref, base_ref, out_ref)


def pair_kernel(mine_ref, received_ref, out_ref):
    out_ref[...] = (mine_ref[...] + received_ref[...].astype(jnp.float32)).astype(out_ref.dtype)


def four_sum_kernel(first, scale_ref, own_ref, two_ref, five_ref, seven_ref, *refs):
    own, two, five, seven = (
        ref[...].astype(jnp.float32) for ref in (own_ref, two_ref, five_ref, seven_ref)
    )
    total = (own + two) + (five + seven)
    if first:
        share_ref, rounded_ref = refs
        total = total * scale_ref[:1]
        share_ref[...] = total
    else:
        previous_ref, rounded_ref = refs
        total = 2.0 * scale_ref[:1] * total - previous_ref[...]
    rounded_ref[...] = total.astype(rounded_ref.dtype)


def next_share_kernel(scale_ref, parts_ref, previous_ref, *out_refs):
    total = 2.0 * scale_ref[:1] * sum_copies(parts_ref) - previous_ref[...]
    copies_ref = out_refs[-1]
    copies_ref[...] = jnp.broadcast_to(total.astype(copies_ref.dtype)[None], copies_ref.shape)
    if len(out_refs) == 2:
        out_refs[0][...] = total


def times_inverse(block, inverse):
    total = None
    for _ in range(3):
        term = inverse.astype(jnp.bfloat16)
        inverse = inverse - term.astype(jnp.float32)
        product = lax.dot_general(
            block, term, (((1,), (1,)), ((), ())), preferred_element_type=jnp.float32
        )
        total = product if total is None else total + product
    return total


def first_gram_kernel(mine_ref, other_ref, out_ref):
    mine, other = flat(mine_ref[...]), flat(other_ref[...])
    pack(contract_rows(mine, mine) + contract_rows(other, other), out_ref)


def second_gram_kernel(parts_ref, mine_ref, other_ref, out_ref, upper_ref, inverse_ref):
    factor(unpack_sum(parts_ref), upper_ref, inverse_ref)
    inverse = inverse_ref[...]
    mine = times_inverse(flat(mine_ref[...]), inverse)
    other = times_inverse(flat(other_ref[...]), inverse)
    pack(gram_of(mine) + gram_of(other), out_ref)


def last_kernel(
    parts_ref, upper_one_ref, inverse_one_ref, block_ref, basis_ref, triangle_ref, upper_ref, inverse_ref
):
    factor(unpack_sum(parts_ref), upper_ref, inverse_ref)
    root = math.sqrt(N)
    first_basis = times_inverse(block_ref[0], inverse_one_ref[...])
    basis_ref[...] = times_transposed(first_basis, inverse_ref[...]) * root
    product = jnp.dot(
        upper_ref[...], upper_one_ref[...], precision=HIGHEST, preferred_element_type=jnp.float32
    )
    triangle_ref[...] = product / root


def swap_core(block):
    return lax.ppermute(block, "core", ((0, 1), (1, 0)))


def swap_row(block, mask):
    count = lax.axis_size("row")
    return lax.ppermute(block, "row", [(i, i ^ mask) for i in range(count)])


def exchange(blocks, axes):
    return lax.all_to_all(blocks, axes, 0, 0, tiled=True)


def body(hamiltonian, start_block, spectral_bound):
    f32, bf16 = jnp.float32, jnp.bfloat16
    block_rows, block_cols = hamiltonian.shape
    row_count = lax.axis_size("row")
    plane_count = lax.axis_size("x") * lax.axis_size("y")
    share = block_rows // (2 * plane_count)
    matrix = hamiltonian.reshape(plane_count, 2, share, block_cols)
    start = start_block.reshape(plane_count, 2, share, K)
    rows = (plane_count, share, K)
    columns = (block_cols // (2 * share), share, K)

    def sum_rows(other, mine_of, previous=None):
        received = swap_row(other, 1)
        (own,) = local_call(pair_kernel, [(columns, bf16)], mine_of(), received, name="pair_row")
        parts = [own, *(swap_row(own, mask) for mask in (2, 5, 7))]
        first = previous is None
        types = [(columns, f32)] * first + [(columns, bf16)]
        args = parts if first else [*parts, previous]
        kernel = functools.partial(four_sum_kernel, first)
        return local_call(kernel, types, scale, *args, name="four_sum")

    def odd_parts(own):
        received = swap_row(own, 1)
        other, mine = local_call(
            odd_first_kernel, [(rows, f32), (rows, f32)], matrix, own, name="odd_first"
        )
        kernels = [functools.partial(odd_last_kernel, offset) for offset in (0, 1)]
        (other,) = local_call(
            kernels[1], [(rows, bf16)], matrix, received, other, name="odd_other"
        )
        swapped = swap_core(other)
        (mine,) = local_call(kernels[0], [(rows, f32)], matrix, received, mine, name="odd_mine")
        (pair,) = local_call(pair_kernel, [(rows, bf16)], mine, swapped, name="pair_core")
        return exchange(pair, PLANE)

    def next_share(parts, previous, keep):
        types = [(previous.shape, f32)] * keep + [(parts.shape, bf16)]
        return local_call(next_share_kernel, types, scale, parts, previous, name="next_share")

    pieces = plane_count // PLANES
    other, mine, zeroth, matrix, scale = local_call(
        start_kernel,
        [(columns, f32), (columns, f32), ((share, K), f32), (matrix.shape, bf16), ((8, K), f32)],
        matrix, start, spectral_bound, name="start", in_spaces=[pltpu.HBM, pltpu.HBM, pltpu.SMEM],
        scratch_shapes=[
            pltpu.VMEM(start.shape, f32), pltpu.VMEM((K, block_cols), f32),
            pltpu.SemaphoreType.DMA((pieces,)), pltpu.SemaphoreType.DMA((pieces,)),
        ],
    )
    first, vectors = sum_rows(other, lambda: mine)
    second, copies = next_share(odd_parts(vectors), zeroth, True)
    own = exchange(copies, PLANE)
    swapped = swap_core(own)

    def even_part(offset):
        kernel = functools.partial(even_kernel, offset)
        dtype = bf16 if offset else f32
        return local_call(kernel, [(columns, dtype)], matrix, own, swapped, name="even")[0]

    (vectors,) = sum_rows(even_part(1), lambda: even_part(0), first)
    (copies,) = next_share(odd_parts(vectors), second, False)

    mine = exchange(copies, PLANE)
    other = swap_core(mine)
    packed = ((row_count, PACK, K), f32)
    square = ((K, K), f32)
    (parts,) = local_call(first_gram_kernel, [packed], mine, other, name="first_gram")
    parts, upper, inverse = local_call(
        second_gram_kernel, [packed, square, square], exchange(parts, "row"), mine, other,
        name="second_gram",
    )
    return local_call(
        last_kernel, [((share, K), f32), square], exchange(parts, "row"), upper, inverse, copies,
        name="last", out_space=jax.ShapeDtypeStruct, scratch_shapes=[pltpu.VMEM((K, K), f32)] * 2,
    )


def solution(mesh):
    rows = mesh.shape["row"]
    torus = jax.sharding.Mesh(mesh.devices.reshape(rows, 4, 4, 2), ("row", "x", "y", "core"))
    col = ("x", "y", "core")
    in_specs = (P("row", col), P("row", None), P())
    out_specs = (P(("row", *col), None), P())
    return jax.shard_map(
        body, mesh=torus, in_specs=in_specs, out_specs=out_specs, check_vma=False
    )
```

```python
import functools
import math

import jax
import jax.numpy as jnp
from jax import lax
from jax.experimental import pallas as pl
from jax.experimental.pallas import tpu as pltpu
from jax.sharding import PartitionSpec as P

N = 32768
K = 128
HALF = K // 2
PACK = HALF + 8
PANEL = 8
HIGHEST = lax.Precision.HIGHEST
VMEM_LIMIT = 24 * 2**20
COLUMNS = 256
CHUNKS = 4
PLANES = 2
PLANE = ("x", "y")


def local_call(
    kernel, out_types, *args, name, in_spaces=None, out_space=pltpu.VMEM, scratch_shapes=()
):
    vmem = pl.BlockSpec(memory_space=pltpu.VMEM)
    in_spaces = in_spaces or [pltpu.VMEM] * len(args)
    return pl.pallas_call(
        kernel,
        in_specs=[pl.BlockSpec(memory_space=space) for space in in_spaces],
        out_specs=[vmem] * len(out_types),
        out_shape=[out_space(*out_type) for out_type in out_types],
        scratch_shapes=list(scratch_shapes),
        compiler_params=pltpu.CompilerParams(vmem_limit_bytes=VMEM_LIMIT),
        name=name,
    )(*(pltpu.with_memory_space_constraint(*pair) for pair in zip(args, in_spaces)))


def contract_rows(left, right):
    return lax.dot_general(
        left, right, (((0,), (0,)), ((), ())), preferred_element_type=jnp.float32
    )


def bf16_terms(block):
    terms = []
    for _ in range(3):
        terms.append(block.astype(jnp.bfloat16))
        block = block - terms[-1].astype(jnp.float32)
    return terms


def gram_of(block):
    high, middle, low = bf16_terms(block)
    wide = contract_rows(high, jnp.concatenate([high, middle], axis=1))
    cross = wide[:, K:] + contract_rows(high, low)
    return wide[:, :K] + (cross + cross.T + contract_rows(middle, middle))


def times_transposed(block, matrix):
    return lax.dot_general(
        block, matrix, (((1,), (1,)), ((), ())), precision=HIGHEST, preferred_element_type=jnp.float32
    )


def factor(gram, upper_ref, inverse_ref):
    count = K // PANEL
    lane = lax.broadcasted_iota(jnp.int32, (PANEL, K), 1)
    sub = lax.broadcasted_iota(jnp.int32, (PANEL, K), 0)
    left = [gram[i * PANEL : (i + 1) * PANEL, :] for i in range(count)]
    right = [jnp.where(lane == sub + i * PANEL, 1.0, 0.0).astype(jnp.float32) for i in range(count)]
    for b in range(count):
        base = b * PANEL
        cols = [
            [
                jnp.broadcast_to(left[i][:, base + k : base + k + 1], (PANEL, K))
                for i in range(b, count)
            ]
            for k in range(PANEL)
        ]
        for k in range(PANEL):
            j = base + k
            pivot = cols[k][0][k : k + 1, :]
            root, reciprocal = lax.rsqrt(pivot), 1.0 / pivot
            left_row = left[b][k : k + 1, :]
            right_row = right[b][k : k + 1, :]
            upper_ref[j : j + 1, :] = jnp.where(lane[:1] >= j, left_row * root, 0.0)
            inverse_ref[j : j + 1, :] = right_row * root
            left_row = left_row * reciprocal
            right_row = right_row * reciprocal
            heads = [cols[m][0][k : k + 1, :] * reciprocal for m in range(k + 1, PANEL)]
            for i in range(b, count):
                col = cols[k][i - b]
                if i == b:
                    if k == PANEL - 1:
                        continue
                    col = jnp.where(sub > k, col, 0.0)
                for m, head in zip(range(k + 1, PANEL), heads):
                    cols[m][i - b] = cols[m][i - b] - col * head
                left[i] = left[i] - col * left_row
                right[i] = right[i] - col * right_row


def grids():
    shape = (HALF, K)
    return lax.broadcasted_iota(jnp.int32, shape, 0), lax.broadcasted_iota(jnp.int32, shape, 1)


def pack(gram, out_ref):
    top, bottom = gram[:HALF], gram[HALF:]
    row, lane = grids()
    triangles = jnp.where(lane >= row, top, pltpu.roll(bottom, HALF, 1))
    diagonal = jnp.sum(jnp.where(lane == row + HALF, bottom, 0.0), axis=0, keepdims=True)
    for i in range(out_ref.shape[0]):
        out_ref[i, :HALF] = triangles
        out_ref[i, HALF:] = jnp.broadcast_to(diagonal, (PACK - HALF, K))


def sum_copies(parts_ref):
    total = parts_ref[0].astype(jnp.float32)
    for i in range(1, parts_ref.shape[0]):
        total = total + parts_ref[i].astype(jnp.float32)
    return total


def unpack_sum(parts_ref):
    packed = sum_copies(parts_ref)
    row, lane = grids()
    triangles, diagonal = packed[:HALF], packed[HALF : HALF + 1]
    last = pltpu.roll(jnp.where(lane < row, triangles, 0.0), HALF, 1)
    strict = jnp.concatenate([jnp.where(lane > row, triangles, 0.0), last], axis=0)
    middle = jnp.concatenate(
        [jnp.where(lane == row, triangles, 0.0), jnp.where(lane == row + HALF, diagonal, 0.0)], axis=0
    )
    return strict + strict.T + middle


def flat(value):
    return value.reshape(-1, value.shape[-1])


def store_row_blocks(product, first, out_ref, base_ref=None):
    rows = out_ref.shape[1]
    for i in range(product.shape[1] // rows):
        block = product[:, i * rows : (i + 1) * rows].T
        if base_ref is not None:
            block = block + base_ref[first + i]
        out_ref[first + i] = block.astype(out_ref.dtype)


def pair_half():
    row = lax.axis_index("row")
    return lax.rem(row + lax.div(row, 4), 2)


def stream_columns(matrix_ref, half, kept_ref, sems):
    width = kept_ref.shape[-1]
    columns = pl.ds(pl.multiple_of(half * width, width), width)
    copies = []
    for n in range(matrix_ref.shape[0] // PLANES):
        part = pl.ds(n * PLANES, PLANES)
        copies.append(
            pltpu.make_async_copy(
                matrix_ref.at[part, :, :, columns], kept_ref.at[part], sems.at[n]
            )
        )
        copies[-1].start()
    return copies


def start_kernel(
    matrix_ref, start_ref, bound_ref, out_ref, vectors_ref, own_ref, kept_ref, scale_ref,
    whole_ref, total_ref, matrix_sems, start_sems,
):
    start_copies = []
    for n in range(start_ref.shape[0] // PLANES):
        part = pl.ds(n * PLANES, PLANES)
        start_copies.append(
            pltpu.make_async_copy(start_ref.at[part], whole_ref.at[part], start_sems.at[n])
        )
        start_copies[-1].start()
    matrix_copies = stream_columns(matrix_ref, 1 - pair_half(), kept_ref, matrix_sems)
    scale_ref[...] = 1.0 / jnp.full(scale_ref.shape, bound_ref[0], jnp.float32)
    for n, copies in enumerate(zip(start_copies, matrix_copies)):
        part = slice(n * PLANES, (n + 1) * PLANES)
        copies[0].wait()
        vectors = whole_ref[part].astype(jnp.bfloat16)
        vectors_ref[part] = vectors
        copies[1].wait()
        product = contract_rows(flat(vectors), flat(kept_ref[part]))
        total_ref[...] = product if n == 0 else total_ref[...] + product
    store_row_blocks(total_ref[...], 0, out_ref)
    plane = lax.axis_index("x") * lax.axis_size("y") + lax.axis_index("y")
    own_ref[...] = whole_ref[plane, lax.axis_index("core")]


def start_own_kernel(matrix_ref, vectors_ref, out_ref, kept_ref, total_ref, sems):
    for n, copy in enumerate(stream_columns(matrix_ref, pair_half(), kept_ref, sems)):
        part = slice(n * PLANES, (n + 1) * PLANES)
        copy.wait()
        product = contract_rows(flat(vectors_ref[part]), flat(kept_ref[part]))
        total_ref[...] = product if n == 0 else total_ref[...] + product
    store_row_blocks(total_ref[...], 0, out_ref)


def even_product(matrix_ref, rows, vectors, base_ref, out_ref):
    for i in range(0, matrix_ref.shape[-1], COLUMNS):
        product = contract_rows(vectors, flat(matrix_ref[:, rows, :, i : i + COLUMNS]))
        store_row_blocks(product, i // out_ref.shape[1], out_ref, base_ref)


def even_first_kernel(pair_ref, matrix_ref, vectors_ref, pair_out_ref, out_ref):
    core, vectors = lax.axis_index("core"), flat(vectors_ref[...])
    even_product(pair_ref, core, vectors, None, pair_out_ref)
    even_product(matrix_ref, core, vectors, None, out_ref)


def even_last_kernel(matrix_ref, vectors_ref, base_ref, out_ref):
    even_product(matrix_ref, 1 - lax.axis_index("core"), flat(vectors_ref[...]), base_ref, out_ref)


def odd_product(offset, matrix_ref, vectors_ref, base_ref, out_ref):
    core = lax.axis_index("core")
    which = core if offset == 0 else 1 - core
    vectors = flat(vectors_ref[...])
    for i in range(0, out_ref.shape[0], CHUNKS):
        rows = flat(matrix_ref[i : i + CHUNKS, which])
        product = jnp.dot(rows, vectors, preferred_element_type=jnp.float32)
        product = product.reshape(CHUNKS, -1, K)
        if base_ref is not None:
            product = product + base_ref[i : i + CHUNKS]
        out_ref[i : i + CHUNKS] = product.astype(out_ref.dtype)


def odd_first_kernel(matrix_ref, vectors_ref, other_ref, mine_ref):
    odd_product(1, matrix_ref, vectors_ref, None, other_ref)
    odd_product(0, matrix_ref, vectors_ref, None, mine_ref)


def odd_last_kernel(offset, matrix_ref, vectors_ref, base_ref, out_ref):
    odd_product(offset, matrix_ref, vectors_ref, base_ref, out_ref)


def pair_kernel(mine_ref, received_ref, out_ref):
    out_ref[...] = (mine_ref[...] + received_ref[...].astype(jnp.float32)).astype(out_ref.dtype)


def four_sum_kernel(first, scale_ref, own_ref, two_ref, five_ref, seven_ref, *refs):
    own, two, five, seven = (
        ref[...].astype(jnp.float32) for ref in (own_ref, two_ref, five_ref, seven_ref)
    )
    total = (own + two) + (five + seven)
    if first:
        share_ref, rounded_ref = refs
        total = total * scale_ref[:1]
        share_ref[...] = total
    else:
        previous_ref, rounded_ref = refs
        total = 2.0 * scale_ref[:1] * total - previous_ref[...]
    rounded_ref[...] = total.astype(rounded_ref.dtype)


def next_share_kernel(scale_ref, parts_ref, previous_ref, *out_refs):
    total = 2.0 * scale_ref[:1] * sum_copies(parts_ref) - previous_ref[...]
    copies_ref = out_refs[-1]
    copies_ref[...] = jnp.broadcast_to(total.astype(copies_ref.dtype)[None], copies_ref.shape)
    if len(out_refs) == 2:
        out_refs[0][...] = total


def times_inverse(block, inverse):
    total = None
    for _ in range(3):
        term = inverse.astype(jnp.bfloat16)
        inverse = inverse - term.astype(jnp.float32)
        product = lax.dot_general(
            block, term, (((1,), (1,)), ((), ())), preferred_element_type=jnp.float32
        )
        total = product if total is None else total + product
    return total


def own_gram_kernel(mine_ref, out_ref):
    mine = flat(mine_ref[...])
    out_ref[...] = contract_rows(mine, mine)


def first_gram_kernel(gram_ref, other_ref, out_ref):
    other = flat(other_ref[...])
    pack(gram_ref[...] + contract_rows(other, other), out_ref)


def second_gram_kernel(parts_ref, mine_ref, other_ref, out_ref, upper_ref, inverse_ref):
    factor(unpack_sum(parts_ref), upper_ref, inverse_ref)
    inverse = inverse_ref[...]
    mine = times_inverse(flat(mine_ref[...]), inverse)
    other = times_inverse(flat(other_ref[...]), inverse)
    pack(gram_of(mine) + gram_of(other), out_ref)


def last_kernel(
    parts_ref, upper_one_ref, inverse_one_ref, block_ref, basis_ref, triangle_ref, upper_ref, inverse_ref
):
    factor(unpack_sum(parts_ref), upper_ref, inverse_ref)
    root = math.sqrt(N)
    first_basis = times_inverse(block_ref[0], inverse_one_ref[...])
    basis_ref[...] = times_transposed(first_basis, inverse_ref[...]) * root
    product = jnp.dot(
        upper_ref[...], upper_one_ref[...], precision=HIGHEST, preferred_element_type=jnp.float32
    )
    triangle_ref[...] = product / root


def swap_core(block):
    return lax.ppermute(block, "core", ((0, 1), (1, 0)))


def swap_row(block, mask):
    count = lax.axis_size("row")
    return lax.ppermute(block, "row", [(i, i ^ mask) for i in range(count)])


def exchange(blocks, axes):
    return lax.all_to_all(blocks, axes, 0, 0, tiled=True)


def body(hamiltonian, start_block, spectral_bound):
    f32, bf16 = jnp.float32, jnp.bfloat16
    block_rows, block_cols = hamiltonian.shape
    row_count = lax.axis_size("row")
    plane_count = lax.axis_size("x") * lax.axis_size("y")
    share = block_rows // (2 * plane_count)
    whole = hamiltonian.reshape(plane_count, 2, share, block_cols)
    start = start_block.reshape(plane_count, 2, share, K)
    rows = (plane_count, share, K)
    half = (block_cols // (2 * share), share, K)
    kept = ((plane_count, 2, share, block_cols // 2), bf16)

    pieces = plane_count // PLANES

    def sum_rows(other, mine_of, previous=None):
        received = swap_row(other, 1)
        (own,) = local_call(pair_kernel, [(half, bf16)], mine_of(), received, name="pair_row")
        parts = [own, *(swap_row(own, mask) for mask in (2, 5, 7))]
        first = previous is None
        types = [(half, f32)] * first + [(half, bf16)]
        args = parts if first else [*parts, previous]
        kernel = functools.partial(four_sum_kernel, first)
        return local_call(kernel, types, scale, *args, name="four_sum")

    def odd_parts(own):
        received = swap_row(own, 1)
        other, mine = local_call(
            odd_first_kernel, [(rows, f32), (rows, f32)], matrix, own, name="odd_first"
        )
        kernels = [functools.partial(odd_last_kernel, offset) for offset in (0, 1)]
        (other,) = local_call(kernels[1], [(rows, bf16)], matrix_pair, received, other, name="odd_other")
        swapped = swap_core(other)
        (mine,) = local_call(kernels[0], [(rows, f32)], matrix_pair, received, mine, name="odd_mine")
        (pair,) = local_call(pair_kernel, [(rows, bf16)], mine, swapped, name="pair_core")
        return exchange(pair, PLANE)

    def next_share(parts, previous, keep):
        types = [(previous.shape, f32)] * keep + [(parts.shape, bf16)]
        return local_call(next_share_kernel, types, scale, parts, previous, name="next_share")

    other, vectors, zeroth, matrix_pair, scale = local_call(
        start_kernel,
        [(half, f32), (start.shape, bf16), ((share, K), f32), kept, ((8, K), f32)],
        whole, start, spectral_bound, name="start",
        in_spaces=[pltpu.HBM, pltpu.HBM, pltpu.SMEM],
        scratch_shapes=[
            pltpu.VMEM(start.shape, f32), pltpu.VMEM((K, block_cols // 2), f32),
            pltpu.SemaphoreType.DMA((pieces,)), pltpu.SemaphoreType.DMA((pieces,)),
        ],
    )
    mine, matrix = local_call(
        start_own_kernel, [(half, f32), kept], whole, vectors, name="start_own",
        in_spaces=[pltpu.HBM, pltpu.VMEM],
        scratch_shapes=[
            pltpu.VMEM((K, block_cols // 2), f32), pltpu.SemaphoreType.DMA((pieces,)),
        ],
    )
    first, vectors = sum_rows(other, lambda: mine)
    second, copies = next_share(odd_parts(vectors), zeroth, True)
    own = exchange(copies, PLANE)
    swapped = swap_core(own)
    other, mine = local_call(
        even_first_kernel, [(half, f32), (half, f32)], matrix_pair, matrix, own, name="even_first"
    )

    def even_last(half_matrix, base, dtype):
        return local_call(
            even_last_kernel, [(half, dtype)], half_matrix, swapped, base, name="even_last"
        )[0]

    other = even_last(matrix_pair, other, bf16)
    (vectors,) = sum_rows(other, lambda: even_last(matrix, mine, f32), first)
    (copies,) = next_share(odd_parts(vectors), second, False)

    mine = exchange(copies, PLANE)
    other = swap_core(mine)
    square = ((K, K), f32)
    (gram,) = local_call(own_gram_kernel, [square], mine, name="own_gram")
    packed = ((row_count, PACK, K), f32)
    (parts,) = local_call(first_gram_kernel, [packed], gram, other, name="first_gram")
    parts, upper, inverse = local_call(
        second_gram_kernel, [packed, square, square], exchange(parts, "row"), mine, other,
        name="second_gram",
    )
    return local_call(
        last_kernel, [((share, K), f32), square], exchange(parts, "row"), upper, inverse, copies,
        name="last", out_space=jax.ShapeDtypeStruct, scratch_shapes=[pltpu.VMEM((K, K), f32)] * 2,
    )


def solution(mesh):
    rows = mesh.shape["row"]
    torus = jax.sharding.Mesh(mesh.devices.reshape(rows, 4, 4, 2), ("row", "x", "y", "core"))
    col = ("x", "y", "core")
    in_specs = (P("row", col), P("row", None), P())
    out_specs = (P(("row", *col), None), P())
    return jax.shard_map(
        body, mesh=torus, in_specs=in_specs, out_specs=out_specs, check_vma=False
    )
```

```python
import functools
import math

import jax
import jax.numpy as jnp
from jax import lax
from jax.experimental import pallas as pl
from jax.experimental.pallas import tpu as pltpu
from jax.sharding import PartitionSpec as P

N = 32768
K = 128
HALF = K // 2
PACK = HALF + 8
PANEL = 8
HIGHEST = lax.Precision.HIGHEST
VMEM_LIMIT = 24 * 2**20
COLUMNS = 256
CHUNKS = 4
PLANES = 2
PLANE = ("x", "y")


def local_call(
    kernel, out_types, *args, name, in_spaces=None, out_space=pltpu.VMEM, scratch_shapes=()
):
    vmem = pl.BlockSpec(memory_space=pltpu.VMEM)
    in_spaces = in_spaces or [pltpu.VMEM] * len(args)
    return pl.pallas_call(
        kernel,
        in_specs=[pl.BlockSpec(memory_space=space) for space in in_spaces],
        out_specs=[vmem] * len(out_types),
        out_shape=[out_space(*out_type) for out_type in out_types],
        scratch_shapes=list(scratch_shapes),
        compiler_params=pltpu.CompilerParams(vmem_limit_bytes=VMEM_LIMIT),
        name=name,
    )(*(pltpu.with_memory_space_constraint(*pair) for pair in zip(args, in_spaces)))


def contract_rows(left, right):
    return lax.dot_general(
        left, right, (((0,), (0,)), ((), ())), preferred_element_type=jnp.float32
    )


def bf16_terms(block):
    terms = []
    for _ in range(3):
        terms.append(block.astype(jnp.bfloat16))
        block = block - terms[-1].astype(jnp.float32)
    return terms


def gram_of(block):
    high, middle, low = bf16_terms(block)
    wide = contract_rows(high, jnp.concatenate([high, middle], axis=1))
    cross = wide[:, K:] + contract_rows(high, low)
    return wide[:, :K] + (cross + cross.T + contract_rows(middle, middle))


def times_transposed(block, matrix):
    return lax.dot_general(
        block, matrix, (((1,), (1,)), ((), ())), precision=HIGHEST, preferred_element_type=jnp.float32
    )


def spread(block, lane):
    return [jnp.broadcast_to(block[:, lane + k : lane + k + 1], block.shape) for k in range(PANEL)]


def factor(gram, upper_ref, inverse_ref):
    count = K // PANEL
    lane = lax.broadcasted_iota(jnp.int32, (PANEL, K), 1)
    sub = lax.broadcasted_iota(jnp.int32, (PANEL, K), 0)
    rows = [gram[i * PANEL : (i + 1) * PANEL, :] for i in range(count)]
    own = spread(rows[0], 0)
    for b in range(count):
        base = b * PANEL
        below = range(b + 1, count)
        cols = {i: spread(rows[i], base) for i in below}
        left = rows[b]
        right = jnp.where(lane < base, left, jnp.where(lane == sub + base, 1.0, 0.0))
        if below:
            ahead, later = spread(left, base + PANEL), spread(rows[b + 1], base + PANEL)
        for i in below:
            rows[i] = jnp.where((lane >= base) & (lane < base + PANEL), 0.0, rows[i])
        for k in range(PANEL):
            j = base + k
            pivot = own[k][k : k + 1, :]
            root, reciprocal = lax.rsqrt(pivot), 1.0 / pivot
            left_row, right_row = left[k : k + 1, :], right[k : k + 1, :]
            upper_ref[j : j + 1, :] = jnp.where(lane[:1] >= j, left_row * root, 0.0)
            inverse_ref[j : j + 1, :] = right_row * root
            left_row, right_row = left_row * reciprocal, right_row * reciprocal
            both = jnp.where(lane[:1] < base + PANEL, right_row, left_row)
            heads = {m: own[m][k : k + 1, :] * reciprocal for m in range(k + 1, PANEL)}
            col = jnp.where(sub > k, own[k], 0.0)
            if below:
                ahead_heads = [block[k : k + 1, :] * reciprocal for block in ahead]
                later = [x - cols[b + 1][k] * head for x, head in zip(later, ahead_heads)]
                ahead = [x - col * head for x, head in zip(ahead, ahead_heads)]
            for m, head in heads.items():
                own[m] = own[m] - col * head
            left, right = left - col * left_row, right - col * right_row
            for i in below:
                col = cols[i][k]
                for m, head in heads.items():
                    cols[i][m] = cols[i][m] - col * head
                rows[i] = rows[i] - col * both
        if below:
            own = later


def grids():
    shape = (HALF, K)
    return lax.broadcasted_iota(jnp.int32, shape, 0), lax.broadcasted_iota(jnp.int32, shape, 1)


def pack(gram, out_ref):
    top, bottom = gram[:HALF], gram[HALF:]
    row, lane = grids()
    triangles = jnp.where(lane >= row, top, pltpu.roll(bottom, HALF, 1))
    diagonal = jnp.sum(jnp.where(lane == row + HALF, bottom, 0.0), axis=0, keepdims=True)
    for i in range(out_ref.shape[0]):
        out_ref[i, :HALF] = triangles
        out_ref[i, HALF:] = jnp.broadcast_to(diagonal, (PACK - HALF, K))


def sum_copies(parts_ref):
    total = parts_ref[0].astype(jnp.float32)
    for i in range(1, parts_ref.shape[0]):
        total = total + parts_ref[i].astype(jnp.float32)
    return total


def unpack_sum(parts_ref):
    packed = sum_copies(parts_ref)
    row, lane = grids()
    triangles, diagonal = packed[:HALF], packed[HALF : HALF + 1]
    last = pltpu.roll(jnp.where(lane < row, triangles, 0.0), HALF, 1)
    strict = jnp.concatenate([jnp.where(lane > row, triangles, 0.0), last], axis=0)
    middle = jnp.concatenate(
        [jnp.where(lane == row, triangles, 0.0), jnp.where(lane == row + HALF, diagonal, 0.0)], axis=0
    )
    return strict + strict.T + middle


def flat(value):
    return value.reshape(-1, value.shape[-1])


def store_row_blocks(product, first, out_ref, base_ref=None):
    rows = out_ref.shape[1]
    for i in range(product.shape[1] // rows):
        block = product[:, i * rows : (i + 1) * rows].T
        if base_ref is not None:
            block = block + base_ref[first + i]
        out_ref[first + i] = block.astype(out_ref.dtype)


def pair_half():
    row = lax.axis_index("row")
    return lax.rem(row + lax.div(row, 4), 2)


def stream_columns(matrix_ref, half, kept_ref, sems):
    width = kept_ref.shape[-1]
    columns = pl.ds(pl.multiple_of(half * width, width), width)
    copies = []
    for n in range(matrix_ref.shape[0] // PLANES):
        part = pl.ds(n * PLANES, PLANES)
        copies.append(
            pltpu.make_async_copy(
                matrix_ref.at[part, :, :, columns], kept_ref.at[part], sems.at[n]
            )
        )
        copies[-1].start()
    return copies


def start_kernel(
    matrix_ref, start_ref, bound_ref, out_ref, vectors_ref, own_ref, kept_ref, scale_ref,
    whole_ref, total_ref, matrix_sems, start_sems,
):
    start_copies = []
    for n in range(start_ref.shape[0] // PLANES):
        part = pl.ds(n * PLANES, PLANES)
        start_copies.append(
            pltpu.make_async_copy(start_ref.at[part], whole_ref.at[part], start_sems.at[n])
        )
        start_copies[-1].start()
    matrix_copies = stream_columns(matrix_ref, 1 - pair_half(), kept_ref, matrix_sems)
    scale_ref[...] = 1.0 / jnp.full(scale_ref.shape, bound_ref[0], jnp.float32)
    for n, copies in enumerate(zip(start_copies, matrix_copies)):
        part = slice(n * PLANES, (n + 1) * PLANES)
        copies[0].wait()
        vectors = whole_ref[part].astype(jnp.bfloat16)
        vectors_ref[part] = vectors
        copies[1].wait()
        product = contract_rows(flat(vectors), flat(kept_ref[part]))
        total_ref[...] = product if n == 0 else total_ref[...] + product
    store_row_blocks(total_ref[...], 0, out_ref)
    plane = lax.axis_index("x") * lax.axis_size("y") + lax.axis_index("y")
    own_ref[...] = whole_ref[plane, lax.axis_index("core")]


def start_own_kernel(matrix_ref, vectors_ref, out_ref, kept_ref, total_ref, sems):
    for n, copy in enumerate(stream_columns(matrix_ref, pair_half(), kept_ref, sems)):
        part = slice(n * PLANES, (n + 1) * PLANES)
        copy.wait()
        product = contract_rows(flat(vectors_ref[part]), flat(kept_ref[part]))
        total_ref[...] = product if n == 0 else total_ref[...] + product
    store_row_blocks(total_ref[...], 0, out_ref)


def even_product(matrix_ref, rows, vectors, base_ref, out_ref):
    for i in range(0, matrix_ref.shape[-1], COLUMNS):
        product = contract_rows(vectors, flat(matrix_ref[:, rows, :, i : i + COLUMNS]))
        store_row_blocks(product, i // out_ref.shape[1], out_ref, base_ref)


def even_first_kernel(pair_ref, matrix_ref, vectors_ref, pair_out_ref, out_ref):
    core, vectors = lax.axis_index("core"), flat(vectors_ref[...])
    even_product(pair_ref, core, vectors, None, pair_out_ref)
    even_product(matrix_ref, core, vectors, None, out_ref)


def even_last_kernel(matrix_ref, vectors_ref, base_ref, out_ref):
    even_product(matrix_ref, 1 - lax.axis_index("core"), flat(vectors_ref[...]), base_ref, out_ref)


def odd_product(offset, matrix_ref, vectors_ref, base_ref, out_ref):
    core = lax.axis_index("core")
    which = core if offset == 0 else 1 - core
    vectors = flat(vectors_ref[...])
    for i in range(0, out_ref.shape[0], CHUNKS):
        rows = flat(matrix_ref[i : i + CHUNKS, which])
        product = jnp.dot(rows, vectors, preferred_element_type=jnp.float32)
        product = product.reshape(CHUNKS, -1, K)
        if base_ref is not None:
            product = product + base_ref[i : i + CHUNKS]
        out_ref[i : i + CHUNKS] = product.astype(out_ref.dtype)


def odd_first_kernel(matrix_ref, vectors_ref, other_ref, mine_ref):
    odd_product(1, matrix_ref, vectors_ref, None, other_ref)
    odd_product(0, matrix_ref, vectors_ref, None, mine_ref)


def odd_last_kernel(offset, matrix_ref, vectors_ref, base_ref, out_ref):
    odd_product(offset, matrix_ref, vectors_ref, base_ref, out_ref)


def pair_kernel(mine_ref, received_ref, *out_refs):
    total = mine_ref[...] + received_ref[...].astype(jnp.float32)
    for out_ref in out_refs:
        out_ref[...] = total.astype(out_ref.dtype)


def four_sum_kernel(first, scale_ref, own_ref, two_ref, five_ref, seven_ref, *refs):
    two, five, seven = (ref[...].astype(jnp.float32) for ref in (two_ref, five_ref, seven_ref))
    total = own_ref[...] + two + (five + seven)
    if first:
        share_ref, rounded_ref = refs
        total = total * scale_ref[:1]
        share_ref[...] = total
    else:
        previous_ref, rounded_ref = refs
        total = 2.0 * scale_ref[:1] * total - previous_ref[...]
    rounded_ref[...] = total.astype(rounded_ref.dtype)


def next_share_kernel(scale_ref, parts_ref, previous_ref, *out_refs):
    total = 2.0 * scale_ref[:1] * sum_copies(parts_ref) - previous_ref[...]
    copies_ref = out_refs[-1]
    copies_ref[...] = jnp.broadcast_to(total.astype(copies_ref.dtype)[None], copies_ref.shape)
    if len(out_refs) == 2:
        out_refs[0][...] = total


def times_inverse(block, inverse):
    total = None
    for _ in range(3):
        term = inverse.astype(jnp.bfloat16)
        inverse = inverse - term.astype(jnp.float32)
        product = lax.dot_general(
            block, term, (((1,), (1,)), ((), ())), preferred_element_type=jnp.float32
        )
        total = product if total is None else total + product
    return total


def own_gram_kernel(mine_ref, out_ref):
    mine = flat(mine_ref[...])
    out_ref[...] = contract_rows(mine, mine)


def first_gram_kernel(gram_ref, other_ref, out_ref):
    other = flat(other_ref[...])
    pack(gram_ref[...] + contract_rows(other, other), out_ref)


def second_gram_kernel(parts_ref, mine_ref, other_ref, out_ref, upper_ref, inverse_ref):
    factor(unpack_sum(parts_ref), upper_ref, inverse_ref)
    inverse = inverse_ref[...]
    mine = times_inverse(flat(mine_ref[...]), inverse)
    other = times_inverse(flat(other_ref[...]), inverse)
    pack(gram_of(mine) + gram_of(other), out_ref)


def last_kernel(
    parts_ref, upper_one_ref, inverse_one_ref, block_ref, basis_ref, triangle_ref, upper_ref, inverse_ref
):
    factor(unpack_sum(parts_ref), upper_ref, inverse_ref)
    root = math.sqrt(N)
    first_basis = times_inverse(block_ref[0], inverse_one_ref[...])
    basis_ref[...] = times_transposed(first_basis, inverse_ref[...]) * root
    product = jnp.dot(
        upper_ref[...], upper_one_ref[...], precision=HIGHEST, preferred_element_type=jnp.float32
    )
    triangle_ref[...] = product / root


def swap_core(block):
    return lax.ppermute(block, "core", ((0, 1), (1, 0)))


def swap_row(block, mask):
    count = lax.axis_size("row")
    return lax.ppermute(block, "row", [(i, i ^ mask) for i in range(count)])


def exchange(blocks, axes):
    return lax.all_to_all(blocks, axes, 0, 0, tiled=True)


def body(hamiltonian, start_block, spectral_bound):
    f32, bf16 = jnp.float32, jnp.bfloat16
    block_rows, block_cols = hamiltonian.shape
    row_count = lax.axis_size("row")
    plane_count = lax.axis_size("x") * lax.axis_size("y")
    share = block_rows // (2 * plane_count)
    whole = hamiltonian.reshape(plane_count, 2, share, block_cols)
    start = start_block.reshape(plane_count, 2, share, K)
    rows = (plane_count, share, K)
    half = (block_cols // (2 * share), share, K)
    kept = ((plane_count, 2, share, block_cols // 2), bf16)

    pieces = plane_count // PLANES

    def sum_rows(other, mine_of, previous=None):
        received = swap_row(other, 1)
        own, rounded = local_call(
            pair_kernel, [(half, f32), (half, bf16)], mine_of(), received, name="pair_row"
        )
        parts = [own, *(swap_row(rounded, mask) for mask in (2, 5, 7))]
        first = previous is None
        types = [(half, f32)] * first + [(half, bf16)]
        args = parts if first else [*parts, previous]
        kernel = functools.partial(four_sum_kernel, first)
        return local_call(kernel, types, scale, *args, name="four_sum")

    def odd_parts(own):
        received = swap_row(own, 1)
        other, mine = local_call(
            odd_first_kernel, [(rows, f32), (rows, f32)], matrix, own, name="odd_first"
        )
        kernels = [functools.partial(odd_last_kernel, offset) for offset in (0, 1)]
        (other,) = local_call(kernels[1], [(rows, bf16)], matrix_pair, received, other, name="odd_other")
        swapped = swap_core(other)
        (mine,) = local_call(kernels[0], [(rows, f32)], matrix_pair, received, mine, name="odd_mine")
        (pair,) = local_call(pair_kernel, [(rows, bf16)], mine, swapped, name="pair_core")
        return exchange(pair, PLANE)

    def next_share(parts, previous, keep):
        types = [(previous.shape, f32)] * keep + [(parts.shape, bf16)]
        return local_call(next_share_kernel, types, scale, parts, previous, name="next_share")

    other, vectors, zeroth, matrix_pair, scale = local_call(
        start_kernel,
        [(half, bf16), (start.shape, bf16), ((share, K), f32), kept, ((8, K), f32)],
        whole, start, spectral_bound, name="start",
        in_spaces=[pltpu.HBM, pltpu.HBM, pltpu.SMEM],
        scratch_shapes=[
            pltpu.VMEM(start.shape, f32), pltpu.VMEM((K, block_cols // 2), f32),
            pltpu.SemaphoreType.DMA((pieces,)), pltpu.SemaphoreType.DMA((pieces,)),
        ],
    )
    mine, matrix = local_call(
        start_own_kernel, [(half, f32), kept], whole, vectors, name="start_own",
        in_spaces=[pltpu.HBM, pltpu.VMEM],
        scratch_shapes=[
            pltpu.VMEM((K, block_cols // 2), f32), pltpu.SemaphoreType.DMA((pieces,)),
        ],
    )
    first, vectors = sum_rows(other, lambda: mine)
    second, copies = next_share(odd_parts(vectors), zeroth, True)
    own = exchange(copies, PLANE)
    swapped = swap_core(own)
    other, mine = local_call(
        even_first_kernel, [(half, f32), (half, f32)], matrix_pair, matrix, own, name="even_first"
    )

    def even_last(half_matrix, base, dtype):
        return local_call(
            even_last_kernel, [(half, dtype)], half_matrix, swapped, base, name="even_last"
        )[0]

    other = even_last(matrix_pair, other, bf16)
    (vectors,) = sum_rows(other, lambda: even_last(matrix, mine, f32), first)
    (copies,) = next_share(odd_parts(vectors), second, False)

    mine = exchange(copies, PLANE)
    other = swap_core(mine)
    square = ((K, K), f32)
    (gram,) = local_call(own_gram_kernel, [square], mine, name="own_gram")
    packed = ((row_count, PACK, K), f32)
    (parts,) = local_call(first_gram_kernel, [packed], gram, other, name="first_gram")
    parts, upper, inverse = local_call(
        second_gram_kernel, [packed, square, square], exchange(parts, "row"), mine, other,
        name="second_gram",
    )
    return local_call(
        last_kernel, [((share, K), f32), square], exchange(parts, "row"), upper, inverse, copies,
        name="last", out_space=jax.ShapeDtypeStruct, scratch_shapes=[pltpu.VMEM((K, K), f32)] * 2,
    )


def solution(mesh):
    rows = mesh.shape["row"]
    torus = jax.sharding.Mesh(mesh.devices.reshape(rows, 4, 4, 2), ("row", "x", "y", "core"))
    col = ("x", "y", "core")
    in_specs = (P("row", col), P("row", None), P())
    out_specs = (P(("row", *col), None), P())
    return jax.shard_map(
        body, mesh=torus, in_specs=in_specs, out_specs=out_specs, check_vma=False
    )
```

```python
import functools
import math

import jax
import jax.numpy as jnp
from jax import lax
from jax.experimental import pallas as pl
from jax.experimental.pallas import tpu as pltpu
from jax.sharding import PartitionSpec as P

N = 32768
K = 128
HALF = K // 2
PACK = HALF + 16
SHARE = PACK // 2
PANEL = 8
HIGHEST = lax.Precision.HIGHEST
VMEM_LIMIT = 24 * 2**20
COLUMNS = 256
CHUNKS = 4
PLANES = 2
PLANE = ("x", "y")


def local_call(
    kernel, out_types, *args, name, in_spaces=None, out_space=pltpu.VMEM, scratch_shapes=()
):
    vmem = pl.BlockSpec(memory_space=pltpu.VMEM)
    in_spaces = in_spaces or [pltpu.VMEM] * len(args)
    return pl.pallas_call(
        kernel,
        in_specs=[pl.BlockSpec(memory_space=space) for space in in_spaces],
        out_specs=[vmem] * len(out_types),
        out_shape=[out_space(*out_type) for out_type in out_types],
        scratch_shapes=list(scratch_shapes),
        compiler_params=pltpu.CompilerParams(vmem_limit_bytes=VMEM_LIMIT),
        name=name,
    )(*(pltpu.with_memory_space_constraint(*pair) for pair in zip(args, in_spaces)))


def contract_rows(left, right):
    return lax.dot_general(
        left, right, (((0,), (0,)), ((), ())), preferred_element_type=jnp.float32
    )


def bf16_terms(block):
    terms = []
    for _ in range(3):
        terms.append(block.astype(jnp.bfloat16))
        block = block - terms[-1].astype(jnp.float32)
    return terms


def gram_of(block):
    high, middle, low = bf16_terms(block)
    wide = contract_rows(high, jnp.concatenate([high, middle], axis=1))
    cross = wide[:, K:] + contract_rows(high, low)
    return wide[:, :K] + (cross + cross.T + contract_rows(middle, middle))


def times_transposed(block, matrix):
    return lax.dot_general(
        block, matrix, (((1,), (1,)), ((), ())), precision=HIGHEST, preferred_element_type=jnp.float32
    )


def spread(block, lane):
    return [jnp.broadcast_to(block[:, lane + k : lane + k + 1], block.shape) for k in range(PANEL)]


def factor(gram, upper_ref, inverse_ref):
    count = K // PANEL
    lane = lax.broadcasted_iota(jnp.int32, (PANEL, K), 1)
    sub = lax.broadcasted_iota(jnp.int32, (PANEL, K), 0)
    rows = [gram[i * PANEL : (i + 1) * PANEL, :] for i in range(count)]
    own = spread(rows[0], 0)
    for b in range(count):
        base = b * PANEL
        below = range(b + 1, count)
        cols = {i: spread(rows[i], base) for i in below}
        left = rows[b]
        right = jnp.where(lane < base, left, jnp.where(lane == sub + base, 1.0, 0.0))
        if below:
            ahead, later = spread(left, base + PANEL), spread(rows[b + 1], base + PANEL)
        for i in below:
            rows[i] = jnp.where((lane >= base) & (lane < base + PANEL), 0.0, rows[i])
        for k in range(PANEL):
            j = base + k
            pivot = own[k][k : k + 1, :]
            root, reciprocal = lax.rsqrt(pivot), 1.0 / pivot
            left_row, right_row = left[k : k + 1, :], right[k : k + 1, :]
            upper_ref[j : j + 1, :] = jnp.where(lane[:1] >= j, left_row * root, 0.0)
            inverse_ref[j : j + 1, :] = right_row * root
            left_row, right_row = left_row * reciprocal, right_row * reciprocal
            both = jnp.where(lane[:1] < base + PANEL, right_row, left_row)
            heads = {m: own[m][k : k + 1, :] * reciprocal for m in range(k + 1, PANEL)}
            col = jnp.where(sub > k, own[k], 0.0)
            if below:
                ahead_heads = [block[k : k + 1, :] * reciprocal for block in ahead]
                later = [x - cols[b + 1][k] * head for x, head in zip(later, ahead_heads)]
                ahead = [x - col * head for x, head in zip(ahead, ahead_heads)]
            for m, head in heads.items():
                own[m] = own[m] - col * head
            left, right = left - col * left_row, right - col * right_row
            for i in below:
                col = cols[i][k]
                for m, head in heads.items():
                    cols[i][m] = cols[i][m] - col * head
                rows[i] = rows[i] - col * both
        if below:
            own = later


def grids():
    shape = (HALF, K)
    return lax.broadcasted_iota(jnp.int32, shape, 0), lax.broadcasted_iota(jnp.int32, shape, 1)


def pack(gram, keep_ref, send_ref):
    top, bottom = gram[:HALF], gram[HALF:]
    row, lane = grids()
    triangles = jnp.where(lane >= row, top, pltpu.roll(bottom, HALF, 1))
    diagonal = jnp.sum(jnp.where(lane == row + HALF, bottom, 0.0), axis=0, keepdims=True)
    packed = jnp.concatenate([triangles, jnp.broadcast_to(diagonal, (PACK - HALF, K))], axis=0)
    core = lax.axis_index("core")
    keep_ref[...] = jnp.where(core == 0, packed[:SHARE], packed[SHARE:])
    send_ref[...] = jnp.where(core == 0, packed[SHARE:], packed[:SHARE])


def sum_copies(parts_ref):
    total = parts_ref[0].astype(jnp.float32)
    for i in range(1, parts_ref.shape[0]):
        total = total + parts_ref[i].astype(jnp.float32)
    return total


def unpack(mine_ref, other_ref):
    core, mine, other = lax.axis_index("core"), mine_ref[...], other_ref[...]
    packed = jnp.concatenate(
        [jnp.where(core == 0, mine, other), jnp.where(core == 0, other, mine)], axis=0
    )
    row, lane = grids()
    triangles, diagonal = packed[:HALF], packed[HALF : HALF + 1]
    last = pltpu.roll(jnp.where(lane < row, triangles, 0.0), HALF, 1)
    strict = jnp.concatenate([jnp.where(lane > row, triangles, 0.0), last], axis=0)
    middle = jnp.concatenate(
        [jnp.where(lane == row, triangles, 0.0), jnp.where(lane == row + HALF, diagonal, 0.0)], axis=0
    )
    return strict + strict.T + middle


def flat(value):
    return value.reshape(-1, value.shape[-1])


def store_row_blocks(product, first, out_ref, base_ref=None):
    rows = out_ref.shape[1]
    for i in range(product.shape[1] // rows):
        block = product[:, i * rows : (i + 1) * rows].T
        if base_ref is not None:
            block = block + base_ref[first + i]
        out_ref[first + i] = block.astype(out_ref.dtype)


def pair_half():
    row = lax.axis_index("row")
    return lax.rem(row + lax.div(row, 4), 2)


def stream_columns(matrix_ref, half, kept_ref, sems):
    width = kept_ref.shape[-1]
    columns = pl.ds(pl.multiple_of(half * width, width), width)
    copies = []
    for n in range(matrix_ref.shape[0] // PLANES):
        part = pl.ds(n * PLANES, PLANES)
        copies.append(
            pltpu.make_async_copy(
                matrix_ref.at[part, :, :, columns], kept_ref.at[part], sems.at[n]
            )
        )
        copies[-1].start()
    return copies


def start_kernel(
    matrix_ref, start_ref, bound_ref, out_ref, vectors_ref, own_ref, kept_ref, scale_ref,
    whole_ref, total_ref, matrix_sems, start_sems,
):
    start_copies = []
    for n in range(start_ref.shape[0] // PLANES):
        part = pl.ds(n * PLANES, PLANES)
        start_copies.append(
            pltpu.make_async_copy(start_ref.at[part], whole_ref.at[part], start_sems.at[n])
        )
        start_copies[-1].start()
    matrix_copies = stream_columns(matrix_ref, 1 - pair_half(), kept_ref, matrix_sems)
    scale_ref[...] = 1.0 / jnp.full(scale_ref.shape, bound_ref[0], jnp.float32)
    for n, copies in enumerate(zip(start_copies, matrix_copies)):
        part = slice(n * PLANES, (n + 1) * PLANES)
        copies[0].wait()
        vectors = whole_ref[part].astype(jnp.bfloat16)
        vectors_ref[part] = vectors
        copies[1].wait()
        product = contract_rows(flat(vectors), flat(kept_ref[part]))
        total_ref[...] = product if n == 0 else total_ref[...] + product
    store_row_blocks(total_ref[...], 0, out_ref)
    plane = lax.axis_index("x") * lax.axis_size("y") + lax.axis_index("y")
    own_ref[...] = whole_ref[plane, lax.axis_index("core")]


def start_own_kernel(matrix_ref, vectors_ref, out_ref, kept_ref, total_ref, sems):
    for n, copy in enumerate(stream_columns(matrix_ref, pair_half(), kept_ref, sems)):
        part = slice(n * PLANES, (n + 1) * PLANES)
        copy.wait()
        product = contract_rows(flat(vectors_ref[part]), flat(kept_ref[part]))
        total_ref[...] = product if n == 0 else total_ref[...] + product
    store_row_blocks(total_ref[...], 0, out_ref)


def even_product(matrix_ref, rows, vectors, base_ref, out_ref):
    for i in range(0, matrix_ref.shape[-1], COLUMNS):
        product = contract_rows(vectors, flat(matrix_ref[:, rows, :, i : i + COLUMNS]))
        store_row_blocks(product, i // out_ref.shape[1], out_ref, base_ref)


def even_first_kernel(pair_ref, matrix_ref, vectors_ref, pair_out_ref, out_ref):
    core, vectors = lax.axis_index("core"), flat(vectors_ref[...])
    even_product(pair_ref, core, vectors, None, pair_out_ref)
    even_product(matrix_ref, core, vectors, None, out_ref)


def even_last_kernel(matrix_ref, vectors_ref, base_ref, out_ref):
    even_product(matrix_ref, 1 - lax.axis_index("core"), flat(vectors_ref[...]), base_ref, out_ref)


def odd_product(offset, matrix_ref, vectors_ref, base_ref, out_ref):
    core = lax.axis_index("core")
    which = core if offset == 0 else 1 - core
    vectors = flat(vectors_ref[...])
    for i in range(0, out_ref.shape[0], CHUNKS):
        rows = flat(matrix_ref[i : i + CHUNKS, which])
        product = jnp.dot(rows, vectors, preferred_element_type=jnp.float32)
        product = product.reshape(CHUNKS, -1, K)
        if base_ref is not None:
            product = product + base_ref[i : i + CHUNKS]
        out_ref[i : i + CHUNKS] = product.astype(out_ref.dtype)


def odd_first_kernel(matrix_ref, vectors_ref, other_ref, mine_ref):
    odd_product(1, matrix_ref, vectors_ref, None, other_ref)
    odd_product(0, matrix_ref, vectors_ref, None, mine_ref)


def odd_last_kernel(offset, matrix_ref, vectors_ref, base_ref, out_ref):
    odd_product(offset, matrix_ref, vectors_ref, base_ref, out_ref)


def pair_kernel(mine_ref, received_ref, *out_refs):
    total = mine_ref[...] + received_ref[...].astype(jnp.float32)
    for out_ref in out_refs:
        out_ref[...] = total.astype(out_ref.dtype)


def four_sum_kernel(first, scale_ref, own_ref, two_ref, five_ref, seven_ref, *refs):
    two, five, seven = (ref[...].astype(jnp.float32) for ref in (two_ref, five_ref, seven_ref))
    total = own_ref[...] + two + (five + seven)
    if first:
        share_ref, rounded_ref = refs
        total = total * scale_ref[:1]
        share_ref[...] = total
    else:
        previous_ref, rounded_ref = refs
        total = 2.0 * scale_ref[:1] * total - previous_ref[...]
    rounded_ref[...] = total.astype(rounded_ref.dtype)


def next_share_kernel(scale_ref, parts_ref, previous_ref, *out_refs):
    total = 2.0 * scale_ref[:1] * sum_copies(parts_ref) - previous_ref[...]
    copies_ref = out_refs[-1]
    copies_ref[...] = jnp.broadcast_to(total.astype(copies_ref.dtype)[None], copies_ref.shape)
    if len(out_refs) == 2:
        out_refs[0][...] = total


def times_inverse(block, inverse):
    total = None
    for _ in range(3):
        term = inverse.astype(jnp.bfloat16)
        inverse = inverse - term.astype(jnp.float32)
        product = lax.dot_general(
            block, term, (((1,), (1,)), ((), ())), preferred_element_type=jnp.float32
        )
        total = product if total is None else total + product
    return total


def first_gram_kernel(block_ref, keep_ref, send_ref):
    block = flat(block_ref[...])
    pack(contract_rows(block, block), keep_ref, send_ref)


def copies_kernel(mine_ref, received_ref, out_ref):
    total = mine_ref[...] + received_ref[...]
    out_ref[...] = jnp.broadcast_to(total[None], out_ref.shape)


def sum_kernel(parts_ref, out_ref):
    out_ref[...] = sum_copies(parts_ref)


def second_gram_kernel(
    mine_ref, other_ref, block_ref, keep_ref, send_ref, upper_ref, inverse_ref
):
    factor(unpack(mine_ref, other_ref), upper_ref, inverse_ref)
    block = times_inverse(flat(block_ref[...]), inverse_ref[...])
    pack(gram_of(block), keep_ref, send_ref)


def last_kernel(
    mine_ref, other_ref, upper_one_ref, inverse_one_ref, block_ref, basis_ref, triangle_ref,
    upper_ref, inverse_ref,
):
    factor(unpack(mine_ref, other_ref), upper_ref, inverse_ref)
    root = math.sqrt(N)
    first_basis = times_inverse(block_ref[0], inverse_one_ref[...])
    basis_ref[...] = times_transposed(first_basis, inverse_ref[...]) * root
    product = jnp.dot(
        upper_ref[...], upper_one_ref[...], precision=HIGHEST, preferred_element_type=jnp.float32
    )
    triangle_ref[...] = product / root


def swap_core(block):
    return lax.ppermute(block, "core", ((0, 1), (1, 0)))


def swap_row(block, mask):
    count = lax.axis_size("row")
    return lax.ppermute(block, "row", [(i, i ^ mask) for i in range(count)])


def exchange(blocks, axes):
    return lax.all_to_all(blocks, axes, 0, 0, tiled=True)


def body(hamiltonian, start_block, spectral_bound):
    f32, bf16 = jnp.float32, jnp.bfloat16
    block_rows, block_cols = hamiltonian.shape
    row_count = lax.axis_size("row")
    plane_count = lax.axis_size("x") * lax.axis_size("y")
    share = block_rows // (2 * plane_count)
    whole = hamiltonian.reshape(plane_count, 2, share, block_cols)
    start = start_block.reshape(plane_count, 2, share, K)
    rows = (plane_count, share, K)
    half = (block_cols // (2 * share), share, K)
    kept = ((plane_count, 2, share, block_cols // 2), bf16)

    pieces = plane_count // PLANES

    def sum_rows(other, mine_of, previous=None):
        received = swap_row(other, 1)
        own, rounded = local_call(
            pair_kernel, [(half, f32), (half, bf16)], mine_of(), received, name="pair_row"
        )
        parts = [own, *(swap_row(rounded, mask) for mask in (2, 5, 7))]
        first = previous is None
        types = [(half, f32)] * first + [(half, bf16)]
        args = parts if first else [*parts, previous]
        kernel = functools.partial(four_sum_kernel, first)
        return local_call(kernel, types, scale, *args, name="four_sum")

    def odd_parts(own):
        received = swap_row(own, 1)
        other, mine = local_call(
            odd_first_kernel, [(rows, f32), (rows, f32)], matrix, own, name="odd_first"
        )
        kernels = [functools.partial(odd_last_kernel, offset) for offset in (0, 1)]
        (other,) = local_call(kernels[1], [(rows, bf16)], matrix_pair, received, other, name="odd_other")
        swapped = swap_core(other)
        (mine,) = local_call(kernels[0], [(rows, f32)], matrix_pair, received, mine, name="odd_mine")
        (pair,) = local_call(pair_kernel, [(rows, bf16)], mine, swapped, name="pair_core")
        return exchange(pair, PLANE)

    def next_share(parts, previous, keep):
        types = [(previous.shape, f32)] * keep + [(parts.shape, bf16)]
        return local_call(next_share_kernel, types, scale, parts, previous, name="next_share")

    other, vectors, zeroth, matrix_pair, scale = local_call(
        start_kernel,
        [(half, bf16), (start.shape, bf16), ((share, K), f32), kept, ((8, K), f32)],
        whole, start, spectral_bound, name="start",
        in_spaces=[pltpu.HBM, pltpu.HBM, pltpu.SMEM],
        scratch_shapes=[
            pltpu.VMEM(start.shape, f32), pltpu.VMEM((K, block_cols // 2), f32),
            pltpu.SemaphoreType.DMA((pieces,)), pltpu.SemaphoreType.DMA((pieces,)),
        ],
    )
    mine, matrix = local_call(
        start_own_kernel, [(half, f32), kept], whole, vectors, name="start_own",
        in_spaces=[pltpu.HBM, pltpu.VMEM],
        scratch_shapes=[
            pltpu.VMEM((K, block_cols // 2), f32), pltpu.SemaphoreType.DMA((pieces,)),
        ],
    )
    first, vectors = sum_rows(other, lambda: mine)
    second, copies = next_share(odd_parts(vectors), zeroth, True)
    own = exchange(copies, PLANE)
    swapped = swap_core(own)
    other, mine = local_call(
        even_first_kernel, [(half, f32), (half, f32)], matrix_pair, matrix, own, name="even_first"
    )

    def even_last(half_matrix, base, dtype):
        return local_call(
            even_last_kernel, [(half, dtype)], half_matrix, swapped, base, name="even_last"
        )[0]

    other = even_last(matrix_pair, other, bf16)
    (vectors,) = sum_rows(other, lambda: even_last(matrix, mine, f32), first)
    (copies,) = next_share(odd_parts(vectors), second, False)

    def sum_gram(keep, send):
        received = swap_core(send)
        (parts,) = local_call(
            copies_kernel, [((row_count, SHARE, K), f32)], keep, received, name="gram_copies"
        )
        (total,) = local_call(sum_kernel, [packed], exchange(parts, "row"), name="gram_sum")
        return total, swap_core(total)

    block = exchange(copies, PLANE)
    packed, square = ((SHARE, K), f32), ((K, K), f32)
    keep, send = local_call(first_gram_kernel, [packed, packed], block, name="first_gram")
    keep, send, upper, inverse = local_call(
        second_gram_kernel, [packed, packed, square, square], *sum_gram(keep, send), block,
        name="second_gram",
    )
    return local_call(
        last_kernel, [((share, K), f32), square], *sum_gram(keep, send), upper, inverse, copies,
        name="last", out_space=jax.ShapeDtypeStruct, scratch_shapes=[pltpu.VMEM((K, K), f32)] * 2,
    )


def solution(mesh):
    rows = mesh.shape["row"]
    torus = jax.sharding.Mesh(mesh.devices.reshape(rows, 4, 4, 2), ("row", "x", "y", "core"))
    col = ("x", "y", "core")
    in_specs = (P("row", col), P("row", None), P())
    out_specs = (P(("row", *col), None), P())
    return jax.shard_map(
        body, mesh=torus, in_specs=in_specs, out_specs=out_specs, check_vma=False
    )
```

```python
import functools
import math

import jax
import jax.numpy as jnp
from jax import lax
from jax.experimental import pallas as pl
from jax.experimental.pallas import tpu as pltpu
from jax.sharding import PartitionSpec as P

N = 32768
K = 128
HALF = K // 2
PACK = HALF + 16
SHARE = PACK // 2
PANEL = 8
HIGHEST = lax.Precision.HIGHEST
VMEM_LIMIT = 24 * 2**20
COLUMNS = 256
CHUNKS = 4
PLANES = 2
PLANE = ("x", "y")


def local_call(
    kernel, out_types, *args, name, in_spaces=None, out_space=pltpu.VMEM, scratch_shapes=()
):
    vmem = pl.BlockSpec(memory_space=pltpu.VMEM)
    in_spaces = in_spaces or [pltpu.VMEM] * len(args)
    return pl.pallas_call(
        kernel,
        in_specs=[pl.BlockSpec(memory_space=space) for space in in_spaces],
        out_specs=[vmem] * len(out_types),
        out_shape=[out_space(*out_type) for out_type in out_types],
        scratch_shapes=list(scratch_shapes),
        compiler_params=pltpu.CompilerParams(vmem_limit_bytes=VMEM_LIMIT),
        name=name,
    )(*(pltpu.with_memory_space_constraint(*pair) for pair in zip(args, in_spaces)))


def contract_rows(left, right):
    return lax.dot_general(
        left, right, (((0,), (0,)), ((), ())), preferred_element_type=jnp.float32
    )


def bf16_terms(block):
    terms = []
    for _ in range(3):
        terms.append(block.astype(jnp.bfloat16))
        block = block - terms[-1].astype(jnp.float32)
    return terms


def gram_of(block):
    high, middle, low = bf16_terms(block)
    wide = contract_rows(high, jnp.concatenate([high, middle], axis=1))
    cross = wide[:, K:] + contract_rows(high, low)
    return wide[:, :K] + (cross + cross.T + contract_rows(middle, middle))


def times_transposed(block, matrix):
    return lax.dot_general(
        block, matrix, (((1,), (1,)), ((), ())), precision=HIGHEST, preferred_element_type=jnp.float32
    )


def spread(block, lane):
    return [jnp.broadcast_to(block[:, lane + k : lane + k + 1], block.shape) for k in range(PANEL)]


def factor(gram, upper_ref, inverse_ref):
    count = K // PANEL
    lane = lax.broadcasted_iota(jnp.int32, (PANEL, K), 1)
    sub = lax.broadcasted_iota(jnp.int32, (PANEL, K), 0)
    rows = [gram[i * PANEL : (i + 1) * PANEL, :] for i in range(count)]
    own = spread(rows[0], 0)
    for b in range(count):
        base = b * PANEL
        below = range(b + 1, count)
        cols = {i: spread(rows[i], base) for i in below}
        left = rows[b]
        right = jnp.where(lane < base, left, jnp.where(lane == sub + base, 1.0, 0.0))
        if below:
            ahead, later = spread(left, base + PANEL), spread(rows[b + 1], base + PANEL)
        for i in below:
            rows[i] = jnp.where((lane >= base) & (lane < base + PANEL), 0.0, rows[i])
        for k in range(PANEL):
            j = base + k
            pivot = own[k][k : k + 1, :]
            root, reciprocal = lax.rsqrt(pivot), 1.0 / pivot
            left_row, right_row = left[k : k + 1, :], right[k : k + 1, :]
            upper_ref[j : j + 1, :] = jnp.where(lane[:1] >= j, left_row * root, 0.0)
            inverse_ref[j : j + 1, :] = right_row * root
            left_row, right_row = left_row * reciprocal, right_row * reciprocal
            both = jnp.where(lane[:1] < base + PANEL, right_row, left_row)
            heads = {m: own[m][k : k + 1, :] * reciprocal for m in range(k + 1, PANEL)}
            col = jnp.where(sub > k, own[k], 0.0)
            if below:
                ahead_heads = [block[k : k + 1, :] * reciprocal for block in ahead]
                later = [x - cols[b + 1][k] * head for x, head in zip(later, ahead_heads)]
                ahead = [x - col * head for x, head in zip(ahead, ahead_heads)]
            for m, head in heads.items():
                own[m] = own[m] - col * head
            left, right = left - col * left_row, right - col * right_row
            for i in below:
                col = cols[i][k]
                for m, head in heads.items():
                    cols[i][m] = cols[i][m] - col * head
                rows[i] = rows[i] - col * both
        if below:
            own = later


def grids():
    shape = (HALF, K)
    return lax.broadcasted_iota(jnp.int32, shape, 0), lax.broadcasted_iota(jnp.int32, shape, 1)


def pack(gram, keep_ref, send_ref):
    top, bottom = gram[:HALF], gram[HALF:]
    row, lane = grids()
    triangles = jnp.where(lane >= row, top, pltpu.roll(bottom, HALF, 1))
    diagonal = jnp.sum(jnp.where(lane == row + HALF, bottom, 0.0), axis=0, keepdims=True)
    packed = jnp.concatenate([triangles, jnp.broadcast_to(diagonal, (PACK - HALF, K))], axis=0)
    core = lax.axis_index("core")
    keep_ref[...] = jnp.where(core == 0, packed[:SHARE], packed[SHARE:])
    send_ref[...] = jnp.where(core == 0, packed[SHARE:], packed[:SHARE])


def sum_copies(parts_ref):
    total = parts_ref[0].astype(jnp.float32)
    for i in range(1, parts_ref.shape[0]):
        total = total + parts_ref[i].astype(jnp.float32)
    return total


def unpack(mine_ref, other_ref):
    core, mine, other = lax.axis_index("core"), mine_ref[...], other_ref[...]
    packed = jnp.concatenate(
        [jnp.where(core == 0, mine, other), jnp.where(core == 0, other, mine)], axis=0
    )
    row, lane = grids()
    triangles, diagonal = packed[:HALF], packed[HALF : HALF + 1]
    last = pltpu.roll(jnp.where(lane < row, triangles, 0.0), HALF, 1)
    strict = jnp.concatenate([jnp.where(lane > row, triangles, 0.0), last], axis=0)
    middle = jnp.concatenate(
        [jnp.where(lane == row, triangles, 0.0), jnp.where(lane == row + HALF, diagonal, 0.0)], axis=0
    )
    return strict + strict.T + middle


def flat(value):
    return value.reshape(-1, value.shape[-1])


def store_row_blocks(product, first, out_ref, base_ref=None):
    rows = out_ref.shape[1]
    for i in range(product.shape[1] // rows):
        block = product[:, i * rows : (i + 1) * rows].T
        if base_ref is not None:
            block = block + base_ref[first + i]
        out_ref[first + i] = block.astype(out_ref.dtype)


def pair_half():
    row = lax.axis_index("row")
    return lax.rem(row + lax.div(row, 4), 2)


def stream_columns(matrix_ref, half, kept_ref, sems):
    width = kept_ref.shape[-1]
    columns = pl.ds(pl.multiple_of(half * width, width), width)
    copies = []
    for n in range(matrix_ref.shape[0] // PLANES):
        part = pl.ds(n * PLANES, PLANES)
        copies.append(
            pltpu.make_async_copy(
                matrix_ref.at[part, :, :, columns], kept_ref.at[part], sems.at[n]
            )
        )
        copies[-1].start()
    return copies


def start_kernel(
    matrix_ref, start_ref, bound_ref, out_ref, vectors_ref, own_ref, kept_ref, scale_ref,
    whole_ref, total_ref, matrix_sems, start_sems,
):
    start_copies = []
    for n in range(start_ref.shape[0] // PLANES):
        part = pl.ds(n * PLANES, PLANES)
        start_copies.append(
            pltpu.make_async_copy(start_ref.at[part], whole_ref.at[part], start_sems.at[n])
        )
        start_copies[-1].start()
    matrix_copies = stream_columns(matrix_ref, 1 - pair_half(), kept_ref, matrix_sems)
    scale_ref[...] = 1.0 / jnp.full(scale_ref.shape, bound_ref[0], jnp.float32)
    for n, copies in enumerate(zip(start_copies, matrix_copies)):
        part = slice(n * PLANES, (n + 1) * PLANES)
        copies[0].wait()
        vectors = whole_ref[part].astype(jnp.bfloat16)
        vectors_ref[part] = vectors
        copies[1].wait()
        product = contract_rows(flat(vectors), flat(kept_ref[part]))
        total_ref[...] = product if n == 0 else total_ref[...] + product
    store_row_blocks(total_ref[...], 0, out_ref)
    plane = lax.axis_index("x") * lax.axis_size("y") + lax.axis_index("y")
    own_ref[...] = whole_ref[plane, lax.axis_index("core")]


def start_own_kernel(matrix_ref, vectors_ref, out_ref, kept_ref, total_ref, sems):
    for n, copy in enumerate(stream_columns(matrix_ref, pair_half(), kept_ref, sems)):
        part = slice(n * PLANES, (n + 1) * PLANES)
        copy.wait()
        product = contract_rows(flat(vectors_ref[part]), flat(kept_ref[part]))
        total_ref[...] = product if n == 0 else total_ref[...] + product
    store_row_blocks(total_ref[...], 0, out_ref)


def even_product(matrix_ref, rows, vectors, base_ref, out_ref):
    for i in range(0, matrix_ref.shape[-1], COLUMNS):
        product = contract_rows(vectors, flat(matrix_ref[:, rows, :, i : i + COLUMNS]))
        store_row_blocks(product, i // out_ref.shape[1], out_ref, base_ref)


def even_first_kernel(pair_ref, matrix_ref, vectors_ref, pair_out_ref, out_ref):
    core, vectors = lax.axis_index("core"), flat(vectors_ref[...])
    even_product(pair_ref, core, vectors, None, pair_out_ref)
    even_product(matrix_ref, core, vectors, None, out_ref)


def even_last_kernel(matrix_ref, vectors_ref, base_ref, out_ref):
    even_product(matrix_ref, 1 - lax.axis_index("core"), flat(vectors_ref[...]), base_ref, out_ref)


def odd_product(offset, matrix_ref, vectors_ref, base_ref, out_ref):
    core = lax.axis_index("core")
    which = core if offset == 0 else 1 - core
    vectors = flat(vectors_ref[...])
    for i in range(0, out_ref.shape[0], CHUNKS):
        rows = flat(matrix_ref[i : i + CHUNKS, which])
        product = jnp.dot(rows, vectors, preferred_element_type=jnp.float32)
        product = product.reshape(CHUNKS, -1, K)
        if base_ref is not None:
            product = product + base_ref[i : i + CHUNKS]
        out_ref[i : i + CHUNKS] = product.astype(out_ref.dtype)


def odd_first_kernel(matrix_ref, vectors_ref, other_ref, mine_ref):
    odd_product(1, matrix_ref, vectors_ref, None, other_ref)
    odd_product(0, matrix_ref, vectors_ref, None, mine_ref)


def odd_last_kernel(offset, matrix_ref, vectors_ref, base_ref, out_ref):
    odd_product(offset, matrix_ref, vectors_ref, base_ref, out_ref)


def pair_kernel(mine_ref, received_ref, *out_refs):
    total = mine_ref[...] + received_ref[...].astype(jnp.float32)
    for out_ref in out_refs:
        out_ref[...] = total.astype(out_ref.dtype)


def four_sum_kernel(first, scale_ref, own_ref, two_ref, five_ref, seven_ref, *refs):
    two, five, seven = (ref[...].astype(jnp.float32) for ref in (two_ref, five_ref, seven_ref))
    total = own_ref[...] + two + (five + seven)
    if first:
        share_ref, rounded_ref = refs
        total = total * scale_ref[:1]
        share_ref[...] = total
    else:
        previous_ref, rounded_ref = refs
        total = 2.0 * scale_ref[:1] * total - previous_ref[...]
    rounded_ref[...] = total.astype(rounded_ref.dtype)


def next_share_kernel(scale_ref, parts_ref, previous_ref, *out_refs):
    total = 2.0 * scale_ref[:1] * sum_copies(parts_ref) - previous_ref[...]
    copies_ref = out_refs[-1]
    copies_ref[...] = jnp.broadcast_to(total.astype(copies_ref.dtype)[None], copies_ref.shape)
    if len(out_refs) == 2:
        out_refs[0][...] = total


def times_inverse(block, inverse):
    total = None
    for _ in range(3):
        term = inverse.astype(jnp.bfloat16)
        inverse = inverse - term.astype(jnp.float32)
        product = lax.dot_general(
            block, term, (((1,), (1,)), ((), ())), preferred_element_type=jnp.float32
        )
        total = product if total is None else total + product
    return total


def first_gram_kernel(block_ref, keep_ref, send_ref):
    block = flat(block_ref[...])
    pack(contract_rows(block, block), keep_ref, send_ref)


def copies_kernel(mine_ref, received_ref, out_ref):
    total = mine_ref[...] + received_ref[...]
    out_ref[...] = jnp.broadcast_to(total[None], out_ref.shape)


def sum_kernel(parts_ref, out_ref):
    out_ref[...] = sum_copies(parts_ref)


def factor_kernel(mine_ref, other_ref, upper_ref, inverse_ref):
    factor(unpack(mine_ref, other_ref), upper_ref, inverse_ref)


def second_gram_kernel(inverse_ref, block_ref, keep_ref, send_ref):
    block = times_inverse(flat(block_ref[...]), inverse_ref[...])
    pack(gram_of(block), keep_ref, send_ref)


def last_kernel(
    mine_ref, other_ref, upper_one_ref, inverse_one_ref, block_ref, basis_ref, triangle_ref,
    upper_ref, inverse_ref,
):
    factor(unpack(mine_ref, other_ref), upper_ref, inverse_ref)
    root = math.sqrt(N)
    first_basis = times_inverse(block_ref[0], inverse_one_ref[...])
    basis_ref[...] = times_transposed(first_basis, inverse_ref[...]) * root
    product = jnp.dot(
        upper_ref[...], upper_one_ref[...], precision=HIGHEST, preferred_element_type=jnp.float32
    )
    triangle_ref[...] = product / root


def swap_core(block):
    return lax.ppermute(block, "core", ((0, 1), (1, 0)))


def swap_row(block, mask):
    count = lax.axis_size("row")
    return lax.ppermute(block, "row", [(i, i ^ mask) for i in range(count)])


def exchange(blocks, axes):
    return lax.all_to_all(blocks, axes, 0, 0, tiled=True)


def body(hamiltonian, start_block, spectral_bound):
    f32, bf16 = jnp.float32, jnp.bfloat16
    block_rows, block_cols = hamiltonian.shape
    row_count = lax.axis_size("row")
    plane_count = lax.axis_size("x") * lax.axis_size("y")
    share = block_rows // (2 * plane_count)
    whole = hamiltonian.reshape(plane_count, 2, share, block_cols)
    start = start_block.reshape(plane_count, 2, share, K)
    rows = (plane_count, share, K)
    half = (block_cols // (2 * share), share, K)
    kept = ((plane_count, 2, share, block_cols // 2), bf16)

    pieces = plane_count // PLANES

    def sum_rows(other, mine_of, previous=None):
        received = swap_row(other, 1)
        own, rounded = local_call(
            pair_kernel, [(half, f32), (half, bf16)], mine_of(), received, name="pair_row"
        )
        parts = [own, *(swap_row(rounded, mask) for mask in (2, 5, 7))]
        first = previous is None
        types = [(half, f32)] * first + [(half, bf16)]
        args = parts if first else [*parts, previous]
        kernel = functools.partial(four_sum_kernel, first)
        return local_call(kernel, types, scale, *args, name="four_sum")

    def odd_parts(own):
        received = swap_row(own, 1)
        other, mine = local_call(
            odd_first_kernel, [(rows, f32), (rows, f32)], matrix, own, name="odd_first"
        )
        kernels = [functools.partial(odd_last_kernel, offset) for offset in (0, 1)]
        (other,) = local_call(kernels[1], [(rows, bf16)], matrix_pair, received, other, name="odd_other")
        swapped = swap_core(other)
        (mine,) = local_call(kernels[0], [(rows, f32)], matrix_pair, received, mine, name="odd_mine")
        (pair,) = local_call(pair_kernel, [(rows, bf16)], mine, swapped, name="pair_core")
        return exchange(pair, PLANE)

    def next_share(parts, previous, keep):
        types = [(previous.shape, f32)] * keep + [(parts.shape, bf16)]
        return local_call(next_share_kernel, types, scale, parts, previous, name="next_share")

    other, vectors, zeroth, matrix_pair, scale = local_call(
        start_kernel,
        [(half, bf16), (start.shape, bf16), ((share, K), f32), kept, ((8, K), f32)],
        whole, start, spectral_bound, name="start",
        in_spaces=[pltpu.HBM, pltpu.HBM, pltpu.SMEM],
        scratch_shapes=[
            pltpu.VMEM(start.shape, f32), pltpu.VMEM((K, block_cols // 2), f32),
            pltpu.SemaphoreType.DMA((pieces,)), pltpu.SemaphoreType.DMA((pieces,)),
        ],
    )
    mine, matrix = local_call(
        start_own_kernel, [(half, f32), kept], whole, vectors, name="start_own",
        in_spaces=[pltpu.HBM, pltpu.VMEM],
        scratch_shapes=[
            pltpu.VMEM((K, block_cols // 2), f32), pltpu.SemaphoreType.DMA((pieces,)),
        ],
    )
    first, vectors = sum_rows(other, lambda: mine)
    second, copies = next_share(odd_parts(vectors), zeroth, True)
    own = exchange(copies, PLANE)
    swapped = swap_core(own)
    other, mine = local_call(
        even_first_kernel, [(half, f32), (half, f32)], matrix_pair, matrix, own, name="even_first"
    )

    def even_last(half_matrix, base, dtype):
        return local_call(
            even_last_kernel, [(half, dtype)], half_matrix, swapped, base, name="even_last"
        )[0]

    other = even_last(matrix_pair, other, bf16)
    (vectors,) = sum_rows(other, lambda: even_last(matrix, mine, f32), first)
    (copies,) = next_share(odd_parts(vectors), second, False)

    def sum_gram(keep, send):
        received = swap_core(send)
        (parts,) = local_call(
            copies_kernel, [((row_count, SHARE, K), f32)], keep, received, name="gram_copies"
        )
        (total,) = local_call(sum_kernel, [packed], exchange(parts, "row"), name="gram_sum")
        return total, swap_core(total)

    block = exchange(copies, PLANE)
    packed, square = ((SHARE, K), f32), ((K, K), f32)
    keep, send = local_call(first_gram_kernel, [packed, packed], block, name="first_gram")
    upper, inverse = local_call(
        factor_kernel, [square, square], *sum_gram(keep, send), name="factor"
    )
    keep, send = local_call(
        second_gram_kernel, [packed, packed], inverse, block, name="second_gram"
    )
    return local_call(
        last_kernel, [((share, K), f32), square], *sum_gram(keep, send), upper, inverse, copies,
        name="last", out_space=jax.ShapeDtypeStruct, scratch_shapes=[pltpu.VMEM((K, K), f32)] * 2,
    )


def solution(mesh):
    rows = mesh.shape["row"]
    torus = jax.sharding.Mesh(mesh.devices.reshape(rows, 4, 4, 2), ("row", "x", "y", "core"))
    col = ("x", "y", "core")
    in_specs = (P("row", col), P("row", None), P())
    out_specs = (P(("row", *col), None), P())
    return jax.shard_map(
        body, mesh=torus, in_specs=in_specs, out_specs=out_specs, check_vma=False
    )
```

```python
import functools
import math

import jax
import jax.numpy as jnp
from jax import lax
from jax.experimental import pallas as pl
from jax.experimental.pallas import tpu as pltpu
from jax.sharding import PartitionSpec as P

N = 32768
K = 128
HALF = K // 2
PACK = HALF + 16
SHARE = PACK // 2
PANEL = 8
HIGHEST = lax.Precision.HIGHEST
VMEM_LIMIT = 24 * 2**20
COLUMNS = 256
CHUNKS = 4
PLANES = 2
SPLIT = 2
PLANE = ("x", "y")


def local_call(
    kernel, out_types, *args, name, in_spaces=None, out_space=pltpu.VMEM, scratch_shapes=()
):
    vmem = pl.BlockSpec(memory_space=pltpu.VMEM)
    in_spaces = in_spaces or [pltpu.VMEM] * len(args)
    return pl.pallas_call(
        kernel,
        in_specs=[pl.BlockSpec(memory_space=space) for space in in_spaces],
        out_specs=[vmem] * len(out_types),
        out_shape=[out_space(*out_type) for out_type in out_types],
        scratch_shapes=list(scratch_shapes),
        compiler_params=pltpu.CompilerParams(vmem_limit_bytes=VMEM_LIMIT),
        name=name,
    )(*(pltpu.with_memory_space_constraint(*pair) for pair in zip(args, in_spaces)))


def contract_rows(left, right):
    return lax.dot_general(
        left, right, (((0,), (0,)), ((), ())), preferred_element_type=jnp.float32
    )


def bf16_terms(block):
    terms = []
    for _ in range(3):
        terms.append(block.astype(jnp.bfloat16))
        block = block - terms[-1].astype(jnp.float32)
    return terms


def gram_of(block):
    high, middle, low = bf16_terms(block)
    wide = contract_rows(high, jnp.concatenate([high, middle], axis=1))
    cross = wide[:, K:] + contract_rows(high, low)
    return wide[:, :K] + (cross + cross.T + contract_rows(middle, middle))


def times_transposed(block, matrix):
    return lax.dot_general(
        block, matrix, (((1,), (1,)), ((), ())), precision=HIGHEST, preferred_element_type=jnp.float32
    )


def spread(block, lane):
    return [jnp.broadcast_to(block[:, lane + k : lane + k + 1], block.shape) for k in range(PANEL)]


def factor(gram, upper_ref, inverse_ref):
    count = K // PANEL
    lane = lax.broadcasted_iota(jnp.int32, (PANEL, K), 1)
    sub = lax.broadcasted_iota(jnp.int32, (PANEL, K), 0)
    rows = [gram[i * PANEL : (i + 1) * PANEL, :] for i in range(count)]
    own = spread(rows[0], 0)
    for b in range(count):
        base = b * PANEL
        below = range(b + 1, count)
        cols = {i: spread(rows[i], base) for i in below}
        left = rows[b]
        right = jnp.where(lane < base, left, jnp.where(lane == sub + base, 1.0, 0.0))
        if below:
            ahead, later = spread(left, base + PANEL), spread(rows[b + 1], base + PANEL)
        for i in below:
            rows[i] = jnp.where((lane >= base) & (lane < base + PANEL), 0.0, rows[i])
        for k in range(PANEL):
            j = base + k
            pivot = own[k][k : k + 1, :]
            root, reciprocal = lax.rsqrt(pivot), 1.0 / pivot
            left_row, right_row = left[k : k + 1, :], right[k : k + 1, :]
            upper_ref[j : j + 1, :] = jnp.where(lane[:1] >= j, left_row * root, 0.0)
            inverse_ref[j : j + 1, :] = right_row * root
            left_row, right_row = left_row * reciprocal, right_row * reciprocal
            both = jnp.where(lane[:1] < base + PANEL, right_row, left_row)
            heads = {m: own[m][k : k + 1, :] * reciprocal for m in range(k + 1, PANEL)}
            col = jnp.where(sub > k, own[k], 0.0)
            if below:
                ahead_heads = [block[k : k + 1, :] * reciprocal for block in ahead]
                later = [x - cols[b + 1][k] * head for x, head in zip(later, ahead_heads)]
                ahead = [x - col * head for x, head in zip(ahead, ahead_heads)]
            for m, head in heads.items():
                own[m] = own[m] - col * head
            left, right = left - col * left_row, right - col * right_row
            for i in below:
                col = cols[i][k]
                for m, head in heads.items():
                    cols[i][m] = cols[i][m] - col * head
                rows[i] = rows[i] - col * both
        if below:
            own = later


def grids():
    shape = (HALF, K)
    return lax.broadcasted_iota(jnp.int32, shape, 0), lax.broadcasted_iota(jnp.int32, shape, 1)


def pack(gram, keep_ref, send_ref):
    top, bottom = gram[:HALF], gram[HALF:]
    row, lane = grids()
    triangles = jnp.where(lane >= row, top, pltpu.roll(bottom, HALF, 1))
    diagonal = jnp.sum(jnp.where(lane == row + HALF, bottom, 0.0), axis=0, keepdims=True)
    packed = jnp.concatenate([triangles, jnp.broadcast_to(diagonal, (PACK - HALF, K))], axis=0)
    core = lax.axis_index("core")
    keep_ref[...] = jnp.where(core == 0, packed[:SHARE], packed[SHARE:])
    send_ref[...] = jnp.where(core == 0, packed[SHARE:], packed[:SHARE])


def sum_copies(parts_ref):
    total = parts_ref[0].astype(jnp.float32)
    for i in range(1, parts_ref.shape[0]):
        total = total + parts_ref[i].astype(jnp.float32)
    return total


def unpack(mine_ref, other_ref):
    core, mine, other = lax.axis_index("core"), mine_ref[...], other_ref[...]
    packed = jnp.concatenate(
        [jnp.where(core == 0, mine, other), jnp.where(core == 0, other, mine)], axis=0
    )
    row, lane = grids()
    triangles, diagonal = packed[:HALF], packed[HALF : HALF + 1]
    last = pltpu.roll(jnp.where(lane < row, triangles, 0.0), HALF, 1)
    strict = jnp.concatenate([jnp.where(lane > row, triangles, 0.0), last], axis=0)
    middle = jnp.concatenate(
        [jnp.where(lane == row, triangles, 0.0), jnp.where(lane == row + HALF, diagonal, 0.0)], axis=0
    )
    return strict + strict.T + middle


def flat(value):
    return value.reshape(-1, value.shape[-1])


def store_row_blocks(product, first, out_ref, base_ref=None):
    rows = out_ref.shape[1]
    for i in range(product.shape[1] // rows):
        block = product[:, i * rows : (i + 1) * rows].T
        if base_ref is not None:
            block = block + base_ref[first + i]
        out_ref[first + i] = block.astype(out_ref.dtype)


def pair_half():
    row = lax.axis_index("row")
    return lax.rem(row + lax.div(row, 4), 2)


def stream_columns(matrix_ref, half, kept_ref, sems):
    width = kept_ref.shape[-1]
    columns = pl.ds(pl.multiple_of(half * width, width), width)
    copies = []
    for n in range(matrix_ref.shape[0] // PLANES):
        part = pl.ds(n * PLANES, PLANES)
        copies.append(
            pltpu.make_async_copy(
                matrix_ref.at[part, :, :, columns], kept_ref.at[part], sems.at[n]
            )
        )
        copies[-1].start()
    return copies


def start_kernel(
    matrix_ref, start_ref, bound_ref, out_ref, vectors_ref, own_ref, kept_ref, scale_ref,
    whole_ref, total_ref, matrix_sems, start_sems,
):
    start_copies = []
    for n in range(start_ref.shape[0] // PLANES):
        part = pl.ds(n * PLANES, PLANES)
        start_copies.append(
            pltpu.make_async_copy(start_ref.at[part], whole_ref.at[part], start_sems.at[n])
        )
        start_copies[-1].start()
    matrix_copies = stream_columns(matrix_ref, 1 - pair_half(), kept_ref, matrix_sems)
    scale_ref[...] = 1.0 / jnp.full(scale_ref.shape, bound_ref[0], jnp.float32)
    for n, copies in enumerate(zip(start_copies, matrix_copies)):
        part = slice(n * PLANES, (n + 1) * PLANES)
        copies[0].wait()
        vectors = whole_ref[part].astype(jnp.bfloat16)
        vectors_ref[part] = vectors
        copies[1].wait()
        product = contract_rows(flat(vectors), flat(kept_ref[part]))
        total_ref[...] = product if n == 0 else total_ref[...] + product
    store_row_blocks(total_ref[...], 0, out_ref)
    plane = lax.axis_index("x") * lax.axis_size("y") + lax.axis_index("y")
    own_ref[...] = whole_ref[plane, lax.axis_index("core")]


def start_own_kernel(matrix_ref, vectors_ref, out_ref, kept_ref, total_ref, sems):
    for n, copy in enumerate(stream_columns(matrix_ref, pair_half(), kept_ref, sems)):
        part = slice(n * PLANES, (n + 1) * PLANES)
        copy.wait()
        product = contract_rows(flat(vectors_ref[part]), flat(kept_ref[part]))
        total_ref[...] = product if n == 0 else total_ref[...] + product
    store_row_blocks(total_ref[...], 0, out_ref)


def even_product(matrix_ref, rows, vectors, base_ref, out_ref):
    for i in range(0, matrix_ref.shape[-1], COLUMNS):
        product = contract_rows(vectors, flat(matrix_ref[:, rows, :, i : i + COLUMNS]))
        store_row_blocks(product, i // out_ref.shape[1], out_ref, base_ref)


def even_first_kernel(pair_ref, matrix_ref, vectors_ref, pair_out_ref, out_ref):
    core, vectors = lax.axis_index("core"), flat(vectors_ref[...])
    even_product(pair_ref, core, vectors, None, pair_out_ref)
    even_product(matrix_ref, core, vectors, None, out_ref)


def even_last_kernel(matrix_ref, vectors_ref, base_ref, out_ref):
    even_product(matrix_ref, 1 - lax.axis_index("core"), flat(vectors_ref[...]), base_ref, out_ref)


def odd_product(offset, matrix_ref, vectors_refs, base_ref, out_ref):
    core = lax.axis_index("core")
    which = core if offset == 0 else 1 - core
    vectors = jnp.concatenate([flat(ref[...]) for ref in vectors_refs], axis=0)
    for i in range(0, out_ref.shape[0], CHUNKS):
        rows = flat(matrix_ref[i : i + CHUNKS, which])
        product = jnp.dot(rows, vectors, preferred_element_type=jnp.float32)
        product = product.reshape(CHUNKS, -1, K)
        if base_ref is not None:
            product = product + base_ref[i : i + CHUNKS]
        out_ref[i : i + CHUNKS] = product.astype(out_ref.dtype)


def odd_first_kernel(matrix_ref, *refs):
    *vectors_refs, other_ref, mine_ref = refs
    odd_product(1, matrix_ref, vectors_refs, None, other_ref)
    odd_product(0, matrix_ref, vectors_refs, None, mine_ref)


def odd_last_kernel(offset, matrix_ref, *refs):
    *vectors_refs, base_ref, out_ref = refs
    odd_product(offset, matrix_ref, vectors_refs, base_ref, out_ref)


def pair_kernel(mine_ref, received_ref, *out_refs):
    total = mine_ref[...] + received_ref[...].astype(jnp.float32)
    first = 0
    for out_ref in out_refs:
        out_ref[...] = total[first : first + out_ref.shape[0]].astype(out_ref.dtype)
        first += out_ref.shape[0]


def pair_row_kernel(mine_ref, received_ref, own_ref, *out_refs):
    pair_kernel(mine_ref, received_ref, *out_refs)
    own_ref[...] = mine_ref[...] + received_ref[...].astype(jnp.float32)


def four_sum_kernel(first, chunk, scale_ref, own_ref, two_ref, five_ref, seven_ref, *refs):
    two, five, seven = (ref[...].astype(jnp.float32) for ref in (two_ref, five_ref, seven_ref))
    blocks = two.shape[0]
    total = own_ref[chunk * blocks : (chunk + 1) * blocks] + two + (five + seven)
    if first:
        share_ref, rounded_ref = refs
        total = total * scale_ref[:1]
        share_ref[...] = total
    else:
        previous_ref, rounded_ref = refs
        total = 2.0 * scale_ref[:1] * total - previous_ref[...]
    rounded_ref[...] = total.astype(rounded_ref.dtype)


def next_share_kernel(scale_ref, parts_ref, previous_ref, *out_refs):
    total = 2.0 * scale_ref[:1] * sum_copies(parts_ref) - previous_ref[...]
    copies_ref = out_refs[-1]
    copies_ref[...] = jnp.broadcast_to(total.astype(copies_ref.dtype)[None], copies_ref.shape)
    if len(out_refs) == 2:
        out_refs[0][...] = total


def times_inverse(block, inverse):
    total = None
    for _ in range(3):
        term = inverse.astype(jnp.bfloat16)
        inverse = inverse - term.astype(jnp.float32)
        product = lax.dot_general(
            block, term, (((1,), (1,)), ((), ())), preferred_element_type=jnp.float32
        )
        total = product if total is None else total + product
    return total


def first_gram_kernel(block_ref, keep_ref, send_ref):
    block = flat(block_ref[...])
    pack(contract_rows(block, block), keep_ref, send_ref)


def copies_kernel(mine_ref, received_ref, out_ref):
    total = mine_ref[...] + received_ref[...]
    out_ref[...] = jnp.broadcast_to(total[None], out_ref.shape)


def sum_kernel(parts_ref, out_ref):
    out_ref[...] = sum_copies(parts_ref)


def factor_kernel(mine_ref, other_ref, upper_ref, inverse_ref):
    factor(unpack(mine_ref, other_ref), upper_ref, inverse_ref)


def second_gram_kernel(inverse_ref, block_ref, keep_ref, send_ref):
    block = times_inverse(flat(block_ref[...]), inverse_ref[...])
    pack(gram_of(block), keep_ref, send_ref)


def last_kernel(
    mine_ref, other_ref, upper_one_ref, inverse_one_ref, block_ref, basis_ref, triangle_ref,
    upper_ref, inverse_ref,
):
    factor(unpack(mine_ref, other_ref), upper_ref, inverse_ref)
    root = math.sqrt(N)
    first_basis = times_inverse(block_ref[0], inverse_one_ref[...])
    basis_ref[...] = times_transposed(first_basis, inverse_ref[...]) * root
    product = jnp.dot(
        upper_ref[...], upper_one_ref[...], precision=HIGHEST, preferred_element_type=jnp.float32
    )
    triangle_ref[...] = product / root


def swap_core(block):
    return lax.ppermute(block, "core", ((0, 1), (1, 0)))


def swap_row(block, mask):
    count = lax.axis_size("row")
    return lax.ppermute(block, "row", [(i, i ^ mask) for i in range(count)])


def exchange(blocks, axes):
    return lax.all_to_all(blocks, axes, 0, 0, tiled=True)


def body(hamiltonian, start_block, spectral_bound):
    f32, bf16 = jnp.float32, jnp.bfloat16
    block_rows, block_cols = hamiltonian.shape
    row_count = lax.axis_size("row")
    plane_count = lax.axis_size("x") * lax.axis_size("y")
    share = block_rows // (2 * plane_count)
    whole = hamiltonian.reshape(plane_count, 2, share, block_cols)
    start = start_block.reshape(plane_count, 2, share, K)
    rows = (plane_count, share, K)
    half = (block_cols // (2 * share), share, K)
    kept = ((plane_count, 2, share, block_cols // 2), bf16)

    pieces = plane_count // PLANES

    chunk_shape = (half[0] // SPLIT, *half[1:])

    def sum_rows(other, mine_of, previous=None):
        received = swap_row(other, 1)
        types = [(half, f32)] + [(chunk_shape, bf16)] * SPLIT
        own, *rounded = local_call(pair_row_kernel, types, mine_of(), received, name="pair_row")
        first = previous is None
        types = [(chunk_shape, f32)] * first + [(chunk_shape, bf16)]
        moved = [[swap_row(block, mask) for mask in (2, 5, 7)] for block in rounded]
        results = []
        for chunk in range(SPLIT):
            args = [own, *moved[chunk]] + ([] if first else [previous[chunk]])
            kernel = functools.partial(four_sum_kernel, first, chunk)
            results.append(local_call(kernel, types, scale, *args, name="four_sum"))
        return zip(*results)

    def odd_parts(own):
        received = [swap_row(block, 1) for block in own]
        other, mine = local_call(
            odd_first_kernel, [(rows, f32), (rows, f32)], matrix, *own, name="odd_first"
        )
        kernels = [functools.partial(odd_last_kernel, offset) for offset in (0, 1)]
        (other,) = local_call(
            kernels[1], [(rows, bf16)], matrix_pair, *received, other, name="odd_other"
        )
        swapped = swap_core(other)
        (mine,) = local_call(kernels[0], [(rows, f32)], matrix_pair, *received, mine, name="odd_mine")
        (pair,) = local_call(pair_kernel, [(rows, bf16)], mine, swapped, name="pair_core")
        return exchange(pair, PLANE)

    def next_share(parts, previous, keep):
        types = [(previous.shape, f32)] * keep + [(parts.shape, bf16)]
        return local_call(next_share_kernel, types, scale, parts, previous, name="next_share")

    other, vectors, zeroth, matrix_pair, scale = local_call(
        start_kernel,
        [(half, bf16), (start.shape, bf16), ((share, K), f32), kept, ((8, K), f32)],
        whole, start, spectral_bound, name="start",
        in_spaces=[pltpu.HBM, pltpu.HBM, pltpu.SMEM],
        scratch_shapes=[
            pltpu.VMEM(start.shape, f32), pltpu.VMEM((K, block_cols // 2), f32),
            pltpu.SemaphoreType.DMA((pieces,)), pltpu.SemaphoreType.DMA((pieces,)),
        ],
    )
    mine, matrix = local_call(
        start_own_kernel, [(half, f32), kept], whole, vectors, name="start_own",
        in_spaces=[pltpu.HBM, pltpu.VMEM],
        scratch_shapes=[
            pltpu.VMEM((K, block_cols // 2), f32), pltpu.SemaphoreType.DMA((pieces,)),
        ],
    )
    first, vectors = sum_rows(other, lambda: mine)
    second, copies = next_share(odd_parts(vectors), zeroth, True)
    own = exchange(copies, PLANE)
    swapped = swap_core(own)
    other, mine = local_call(
        even_first_kernel, [(half, f32), (half, f32)], matrix_pair, matrix, own, name="even_first"
    )

    def even_last(half_matrix, base, dtype):
        return local_call(
            even_last_kernel, [(half, dtype)], half_matrix, swapped, base, name="even_last"
        )[0]

    other = even_last(matrix_pair, other, bf16)
    (vectors,) = sum_rows(other, lambda: even_last(matrix, mine, f32), first)
    (copies,) = next_share(odd_parts(vectors), second, False)

    def sum_gram(keep, send):
        received = swap_core(send)
        (parts,) = local_call(
            copies_kernel, [((row_count, SHARE, K), f32)], keep, received, name="gram_copies"
        )
        (total,) = local_call(sum_kernel, [packed], exchange(parts, "row"), name="gram_sum")
        return total, swap_core(total)

    block = exchange(copies, PLANE)
    packed, square = ((SHARE, K), f32), ((K, K), f32)
    keep, send = local_call(first_gram_kernel, [packed, packed], block, name="first_gram")
    upper, inverse = local_call(
        factor_kernel, [square, square], *sum_gram(keep, send), name="factor"
    )
    keep, send = local_call(
        second_gram_kernel, [packed, packed], inverse, block, name="second_gram"
    )
    return local_call(
        last_kernel, [((share, K), f32), square], *sum_gram(keep, send), upper, inverse, copies,
        name="last", out_space=jax.ShapeDtypeStruct, scratch_shapes=[pltpu.VMEM((K, K), f32)] * 2,
    )


def solution(mesh):
    rows = mesh.shape["row"]
    torus = jax.sharding.Mesh(mesh.devices.reshape(rows, 4, 4, 2), ("row", "x", "y", "core"))
    col = ("x", "y", "core")
    in_specs = (P("row", col), P("row", None), P())
    out_specs = (P(("row", *col), None), P())
    return jax.shard_map(
        body, mesh=torus, in_specs=in_specs, out_specs=out_specs, check_vma=False
    )
```
